256 devices in a mesh: rows: 32 (over x, y, core), cols: 8 (over z).
Axes of the slice: x: 4, y: 4, z: 8, core: 2. Of those that a mesh axis runs over, the one named last changes fastest.
Arguments:
- fblocks: bfloat16 [512, 20, 128, 128], P('rows'), may hold values from -0.15625 to 0.15625
- fcol: int32 [512, 20], P('rows'), may hold values from 0 to 511, as said below
- zblocks: bfloat16 [512, 8, 128, 128], P('rows', 'cols'), may hold values from -0.5 to 0.5
- zcol: int32 [512, 8], P('rows', 'cols'), may hold values from 0 to 1, as said below
Outputs:
- f_orth: float32 [2048, 2048], P('rows', 'cols')
The draws below stay inside these ranges and needn't reach their ends.
Inputs may be any that keep to these rules, and one draw needn't show every extreme that they name: `fcol`: each block row r lists 20 distinct block rows; the first is r itself, every other g satisfies (g - r) mod 512 <= 48 or (r - g) mod 512 <= 48. `zcol`: within a block row, the 1 entries of one group are distinct.
All inputs are finite; a program needn't handle non-finite values.
Results may differ from the reference program's by a relative error of at most 0.0029.
Values may be sent and summed in bfloat16 or wider, within the bound.
A program may use at most 128 MiB of HBM per device.

```python
import jax
import jax.numpy as jnp
from jax import lax

B = 128
K = 20
S = 1
REACH = 3
RB_DEV = 16
CB = 2
NB = 512
NC = 16
N_COLS = 8


def draw_fcol(key, part):
    key = jax.random.fold_in(key, 11)
    distance = REACH * RB_DEV
    row_keys = jax.random.split(key, NB)

    def pick_row(row_key):
        return jax.random.permutation(row_key, 2 * distance)[:K - 1]
    picks = jax.vmap(pick_row)(row_keys).astype(jnp.int32)
    offsets = jnp.where(picks < distance, picks + 1, distance - 1 - picks)
    offsets = jnp.concatenate([jnp.zeros((NB, 1), jnp.int32), offsets], axis=1)
    row_index = jnp.arange(NB, dtype=jnp.int32)[:, None]
    return jnp.mod(row_index + offsets, NB).astype(jnp.int32)


def draw_zcol(key, part):
    key = jax.random.fold_in(key, 23)
    group_keys = jax.random.split(key, NB * N_COLS)

    def pick_group(group_key):
        return jax.random.permutation(group_key, CB)[:S]
    picks = jax.vmap(pick_group)(group_keys).astype(jnp.int32)
    return picks.reshape(NB, N_COLS * S)


def shard_levels(rng, dims, pieces, least, top_value):
    def one(dim, blocks):
        heights = jax.random.uniform(jax.random.fold_in(jax.random.fold_in(rng, 6), dim), (blocks,), jnp.float32, least / len(pieces), top_value / len(pieces))
        return jnp.repeat(jnp.exp(heights), dims[dim] // blocks).reshape((-1,) + (1,) * (len(dims) - dim - 1))

    loudness = one(*pieces[0])
    for cut in pieces[1:]:
        loudness = loudness * one(*cut)
    return loudness


def bell_draw(rng, shape, width, bound, cuts=(), kind=jnp.bfloat16):
    array = jax.random.normal(rng, shape, jnp.float32) * width
    if len(cuts) > 0:
        array = shard_levels(rng, shape, cuts, -0.22, 0.18) * array
    return jnp.clip(array, min=-bound, max=bound).astype(kind)


def setup_inputs(seed: int = 0) -> dict:
    key_of = jax.random.split(jax.random.key(seed), 5)
    fblocks = bell_draw(key_of[0], (NB, K, B, B), (K * B * S // CB) ** -0.5, 0.15625, ((0, 32),))
    fcol = draw_fcol(jax.random.fold_in(key_of[4], 71), 0)
    zblocks = bell_draw(key_of[2], (NB, N_COLS * S, B, B), B ** -0.5, 0.5, ((0, 32), (1, 8)))
    zcol = draw_zcol(jax.random.fold_in(key_of[4], 71), 0)
    return {"fblocks": fblocks, "fcol": fcol, "zblocks": zblocks, "zcol": zcol}


def reference(fblocks, fcol, zblocks, zcol):
    group_base = (jnp.arange(N_COLS * S, dtype=jnp.int32) // S) * CB
    global_cols = (zcol + group_base[None, :]).astype(jnp.int32)
    zwide = zblocks.astype(jnp.float32)

    def product_row(inputs):
        frow, columns = inputs
        picked = zwide[columns]
        products = jnp.einsum('kab,kmbe->kmae', frow.astype(jnp.float32), picked)
        targets = global_cols[columns].reshape(-1)
        summed = jnp.zeros((NC, B, B), jnp.float32).at[targets].add(products.reshape(-1, B, B))
        return summed.astype(jnp.bfloat16)

    product = lax.map(product_row, (fblocks, fcol))

    def accumulate(total, inputs):
        zrow, columns, fzrow = inputs
        terms = jnp.einsum('mab,cae->mbce', zrow.astype(jnp.float32), fzrow.astype(jnp.float32))
        return total.at[columns].add(terms), None

    start_total = jnp.zeros((NC, B, NC, B), jnp.float32)
    total, _ = lax.scan(accumulate, start_total, (zblocks, global_cols, product))
    return total.reshape(NC * B, NC * B)
```

```python
import jax
import jax.numpy as jnp
from jax import lax
from jax.experimental import pallas as pl
from jax.experimental.pallas import tpu as pltpu
from jax.sharding import PartitionSpec as P

B = 128
K = 20
CB = 2
ROWS = 16
CHIPS = 16
GROUPS = 8
NB = 512
SLOTS = 7
OWN = 3
HALF = ROWS // 2
WIDE = CB * B
OUT = 64
ORDER = (0, -1, 1, -2, 2, -3, 3, 4)
MESH = pl.DeviceIdType.MESH
F32 = jnp.float32
BF16 = jnp.bfloat16


def kernel(
    fcol_hbm,
    zcol_hbm,
    f_hbm,
    z_hbm,
    out,
    fv,
    halo,
    zexp,
    ring,
    tags,
    wide,
    turned,
    masks,
    part,
    other,
    chip_sum,
    arrived,
    total,
    fcol,
    zcol,
    small_sem,
    z_sem,
    f_sem,
    halo_send,
    halo_recv,
    ring_send,
    ring_recv,
    tag_send,
    tag_recv,
    pair_send,
    pair_recv,
    sum_send,
    sum_recv,
):
    r = lax.axis_index("rows")
    z = lax.axis_index("cols")
    m = lax.div(r, 2)
    q = lax.rem(r, 2)
    s = 2 * q - 1

    def chip(step):
        return lax.rem(m + step + 2 * CHIPS, CHIPS)

    def group(step):
        return lax.rem(z + step + 2 * GROUPS, GROUPS)

    sibling = (r - s, z)

    load_z = []
    for half in range(2):
        load_z.append(
            pltpu.make_async_copy(
                z_hbm.at[pl.ds(half * HALF * B, HALF * B)],
                halo.at[OWN, half, pl.ds(0, HALF * B)],
                z_sem.at[half],
            )
        )
        load_z[-1].start()
    load_zcol = pltpu.make_async_copy(zcol_hbm, zcol, small_sem.at[0])
    load_zcol.start()
    load_fcol = pltpu.make_async_copy(fcol_hbm, fcol, small_sem.at[1])
    load_fcol.start()
    load_f = []
    for g in range(4):
        rows = pl.ds(4 * g, 4)
        load_f.append(pltpu.make_async_copy(f_hbm.at[rows], fv.at[rows], f_sem.at[g]))
        load_f[-1].start()

    barrier = pltpu.get_barrier_semaphore()
    peers = [(r, group(1)), (r, group(-1)), sibling, (2 * chip(s) + 1 - q, z)]
    peers += [(2 * chip(j) + q, z) for j in range(1, CHIPS)]
    for peer in peers:
        pl.semaphore_signal(barrier, inc=1, device_id=peer, device_id_type=MESH)

    def remote(src, dst, send, recv, device):
        return pltpu.make_async_remote_copy(
            src_ref=src, dst_ref=dst, send_sem=send, recv_sem=recv,
            device_id=device, device_id_type=MESH,
        )

    sent = []

    def go(copy):
        copy.start()
        sent.append(copy)

    def drain(count):
        for copy in sent[:count]:
            copy.wait_send()
        del sent[:count]

    def ring_copy(sense, distance, half):
        n = group(-sense * (distance - 1))
        at = (0 if sense == 1 else 1, distance - 1, half)
        if distance == 1:
            source = z_hbm.at[pl.ds(half * HALF * B, HALF * B)]
        else:
            source = ring.at[n, half]
        return remote(
            source, ring.at[n, half], ring_send.at[at], ring_recv.at[at], (r, group(sense))
        )

    def ring_wait(sense, distance, half):
        n = group(-sense * distance)
        at = (0 if sense == 1 else 1, distance - 1, half)
        remote(
            ring.at[n, half], ring.at[n, half], ring_send.at[at], ring_recv.at[at],
            (r, group(sense)),
        ).wait_recv()

    def tag_copy(sense, distance):
        n = group(-sense * (distance - 1))
        at = (0 if sense == 1 else 1, distance - 1)
        return remote(
            tags.at[n], tags.at[n], tag_send.at[at], tag_recv.at[at], (r, group(sense))
        )

    def tag_wait(sense, distance):
        n = group(-sense * distance)
        at = (0 if sense == 1 else 1, distance - 1)
        remote(
            tags.at[n], tags.at[n], tag_send.at[at], tag_recv.at[at], (r, group(sense))
        ).wait_recv()

    pl.semaphore_wait(barrier, len(peers))
    go(ring_copy(1, 1, 0))
    go(ring_copy(-1, 1, 1))

    load_zcol.wait()
    load_fcol.wait()
    row_of = lax.broadcasted_iota(jnp.int32, (ROWS, B), 0)

    def mask_tile(first):
        tile = jnp.zeros((ROWS, B), F32)
        for i in range(first, ROWS):
            tile = jnp.where(row_of == i - first, zcol[0, i].astype(F32), tile)
        return tile.astype(BF16)

    tags[z] = mask_tile(0)
    halo[OWN, 0, pl.ds(HALF * B, ROWS)] = mask_tile(0)
    halo[OWN, 1, pl.ds(HALF * B, ROWS)] = mask_tile(HALF)
    for half in range(2):
        load_z[half].wait()

    def halo_copy(step, order, src_slot, dst_slot, device, core=q):
        half = core if order == 0 else 1 - core
        return remote(
            halo.at[src_slot, half], halo.at[dst_slot, half],
            halo_send.at[step, order], halo_recv.at[step, order], device,
        )

    def halo_wait(step, order, slot):
        halo_copy(step, order, slot, slot, sibling, q if step < 2 else 1 - q).wait_recv()

    for order in range(2):
        go(halo_copy(0, order, OWN, 1, (2 * chip(1) + q, z)))
        go(halo_copy(1, order, OWN, 5, (2 * chip(-1) + q, z)))
    for order in range(2):
        go(halo_copy(2, order, OWN, 3 + s, sibling))
    go(ring_copy(1, 1, 1))
    go(ring_copy(-1, 1, 0))
    go(tag_copy(1, 1))
    go(tag_copy(-1, 1))

    def expand_slot(slot, half):
        masks[...] = halo[slot, half, pl.ds(HALF * B, ROWS)].astype(F32)

        @pl.loop(0, HALF)
        def _(j):
            block = halo[slot, half, pl.ds(pl.multiple_of(j * B, B), B)].astype(F32)
            second = masks[pl.ds(j, 1), :]
            at = slot * ROWS + half * HALF + j
            zexp[at, :, 0:B] = (block * (1.0 - second)).astype(BF16)
            zexp[at, :, B:WIDE] = (block * second).astype(BF16)

    def expand_both(slot):
        expand_slot(slot, 0)
        expand_slot(slot, 1)

    expand_both(OWN)
    halo_wait(2, 0, 3 - s)
    halo_wait(2, 1, 3 - s)
    expand_both(3 - s)

    def expand_half(t, half):
        n = group(ORDER[t])
        masks[...] = tags[n].astype(F32)

        @pl.loop(0, HALF)
        def _(j):
            block = ring[n, half, pl.ds(pl.multiple_of(j * B, B), B)].astype(F32)
            second = masks[pl.ds(half * HALF + j, 1), :]
            rows = pl.ds(pl.multiple_of((half * HALF + j) * B, B), B)
            wide[t, rows, 0:B] = (block * (1.0 - second)).astype(BF16)
            wide[t, rows, B:WIDE] = (block * second).astype(BF16)

    def forward(distance, first):
        right, left = (0, 1) if first else (1, 0)
        for sense, half in ((1, right), (-1, left)):
            ring_wait(sense, distance, half)
            if distance < 3 or (distance == 3 and first):
                go(ring_copy(sense, distance + 1, half))
            if first:
                tag_wait(sense, distance)
                if distance < 3 or sense == 1:
                    go(tag_copy(sense, distance + 1))
        expand_half(2 * distance - 1, right)
        expand_half(2 * distance, left)

    def halo_forward(order):
        halo_wait(0, order, 1)
        halo_wait(1, order, 5)
        go(halo_copy(5, order, 3 - 2 * s, 3 - 3 * s, (2 * chip(s) + 1 - q, z)))
        go(halo_copy(3, order, 1, 1 + s, sibling))
        go(halo_copy(4, order, 5, 5 + s, sibling))

    forward(1, True)
    halo_forward(0)
    forward(1, False)
    halo_forward(1)
    expand_both(1)
    expand_both(5)
    for order in range(2):
        halo_wait(3, order, 1 - s)
        halo_wait(4, order, 5 - s)
    expand_both(1 - s)
    expand_both(5 - s)

    first_row = (r - OWN) * ROWS

    def place(column):
        return jnp.minimum(lax.rem(column - first_row + NB, NB), SLOTS * ROWS - 1)

    def product_row(i):
        left = jnp.concatenate([fv[i, pl.ds(k * B, B)] for k in range(K)], axis=1)
        right = jnp.concatenate([zexp[place(fcol[i, k])] for k in range(K)], axis=0)
        acc = jnp.dot(left, right, preferred_element_type=F32)
        rows = pl.ds(pl.multiple_of(i * B, B), B)
        for c in range(CB):
            turned[c * B:(c + 1) * B, rows] = jnp.transpose(acc[:, c * B:(c + 1) * B]).astype(BF16)

    def product_rows(first):
        for i in range(4):
            product_row(first + i)

    for g in range(4):
        load_f[g].wait()
    near = HALF * (1 - q)
    halo_wait(5, 0, 3 + 3 * s)
    expand_slot(3 + 3 * s, 1 - q)
    product_rows(near)
    forward(2, True)
    product_rows(near + 4)
    halo_wait(5, 1, 3 + 3 * s)
    expand_slot(3 + 3 * s, q)
    product_rows(HALF * q)
    forward(2, False)
    product_rows(HALF * q + 4)

    def group_of(t):
        return group(ORDER[t])

    pair_copies = []

    def window(t):
        right = wide[t]
        if t == 0:
            right = zexp[OWN * ROWS:(OWN + 1) * ROWS].reshape(ROWS * B, WIDE)
        product = jnp.transpose(jnp.dot(turned[...], right, preferred_element_type=F32))
        for b in range(4):
            part[t, b % 2, b // 2] = product[b * OUT:(b + 1) * OUT]
        copy = remote(
            part.at[t, 1 - q], other.at[t], pair_send.at[t], pair_recv.at[t], sibling
        )
        pair_copies.append(copy)
        go(copy)

    def sum_copy(t, h):
        d = 2 * group_of(t) + h
        return d, remote(
            chip_sum.at[t, h], arrived.at[m], sum_send.at[t, h], sum_recv.at[m],
            (2 * d + q, z),
        )

    def finish(t):
        pair_copies[t].wait_recv()
        for h in range(2):
            both = part[t, q, h] + other[t, h]
            chip_sum[t, h] = both.astype(BF16)
            d, copy = sum_copy(t, h)

            @pl.when(d == m)
            def _():
                total[...] = both

            @pl.when(d != m)
            def _():
                copy.start()

    window(0)
    window(1)
    finish(0)
    window(2)
    finish(1)
    early = len(sent)
    forward(3, True)
    window(3)
    finish(2)
    window(4)
    finish(3)
    finish(4)
    forward(3, False)
    window(5)
    window(6)
    finish(5)
    finish(6)
    drain(early)
    tag_wait(1, 4)
    ring_wait(1, 4, 0)
    ring_wait(-1, 4, 1)
    expand_half(7, 0)
    expand_half(7, 1)
    window(7)
    finish(7)

    acc = total[...]
    for j in range(1, CHIPS):
        source = chip(j)
        remote(
            arrived.at[source], arrived.at[source], sum_send.at[0, 0], sum_recv.at[source], sibling
        ).wait_recv()
        acc += arrived[source].astype(F32)
    out[...] = acc

    drain(len(sent))
    for t in range(GROUPS):
        for h in range(2):
            d, copy = sum_copy(t, h)

            @pl.when(d != m)
            def _():
                copy.wait_send()


def body(fblocks, fcol, zblocks, zcol):
    dma = pltpu.SemaphoreType.DMA
    return pl.pallas_call(
        kernel,
        out_shape=jax.ShapeDtypeStruct((OUT, WIDE), F32),
        in_specs=[pl.BlockSpec(memory_space=pl.ANY)] * 4,
        out_specs=pl.BlockSpec(memory_space=pltpu.VMEM),
        scratch_shapes=[
            pltpu.VMEM((ROWS, K * B, B), BF16),
            pltpu.VMEM((SLOTS, 2, HALF * B + ROWS, B), BF16),
            pltpu.VMEM((SLOTS * ROWS, B, WIDE), BF16),
            pltpu.VMEM((GROUPS, 2, HALF * B, B), BF16),
            pltpu.VMEM((GROUPS, ROWS, B), BF16),
            pltpu.VMEM((GROUPS, ROWS * B, WIDE), BF16),
            pltpu.VMEM((WIDE, ROWS * B), BF16),
            pltpu.VMEM((ROWS, B), F32),
            pltpu.VMEM((GROUPS, 2, 2, OUT, WIDE), F32),
            pltpu.VMEM((GROUPS, 2, OUT, WIDE), F32),
            pltpu.VMEM((GROUPS, 2, OUT, WIDE), BF16),
            pltpu.VMEM((CHIPS, OUT, WIDE), BF16),
            pltpu.VMEM((OUT, WIDE), F32),
            pltpu.SMEM((ROWS, K), jnp.int32),
            pltpu.SMEM((1, ROWS), jnp.int32),
            dma((2,)),
            dma((2,)),
            dma((4,)),
            dma((6, 2)),
            dma((6, 2)),
            dma((2, 4, 2)),
            dma((2, 4, 2)),
            dma((2, 4)),
            dma((2, 4)),
            dma((GROUPS,)),
            dma((GROUPS,)),
            dma((GROUPS, 2)),
            dma((CHIPS,)),
        ],
        compiler_params=pltpu.CompilerParams(
            collective_id=0, has_side_effects=True, vmem_limit_bytes=60 * 2**20
        ),
    )(
        fcol,
        zcol.reshape(1, ROWS),
        fblocks.reshape(ROWS, K * B, B),
        zblocks.reshape(ROWS * B, B),
    )


def solution(mesh):
    in_specs = (
        P("rows", None, None, None),
        P("rows", None),
        P("rows", "cols", None, None),
        P("rows", "cols"),
    )
    out_specs = P("rows", "cols")
    return jax.shard_map(body, mesh=mesh, in_specs=in_specs, out_specs=out_specs, check_vma=False)
```

```python
import jax
import jax.numpy as jnp
from jax import lax
from jax.experimental import pallas as pl
from jax.experimental.pallas import tpu as pltpu
from jax.sharding import PartitionSpec as P

B = 128
K = 20
CB = 2
ROWS = 16
CHIPS = 16
GROUPS = 8
NB = 512
SLOTS = 7
OWN = 3
HALF = ROWS // 2
WIDE = CB * B
OUT = 64
ORDER = (0, -1, 1, -2, 2, -3, 3, 4)
MESH = pl.DeviceIdType.MESH
F32 = jnp.float32
BF16 = jnp.bfloat16


def kernel(
    fcol_hbm,
    zcol_hbm,
    f_hbm,
    z_hbm,
    out,
    fv,
    halo,
    zexp,
    ring,
    tags,
    wide,
    turned,
    masks,
    part,
    other,
    chip_sum,
    arrived,
    total,
    fcol,
    zcol,
    small_sem,
    z_sem,
    f_sem,
    halo_send,
    halo_recv,
    ring_send,
    ring_recv,
    tag_send,
    tag_recv,
    pair_send,
    pair_recv,
    sum_send,
    sum_recv,
):
    r = lax.axis_index("rows")
    z = lax.axis_index("cols")
    m = lax.div(r, 2)
    q = lax.rem(r, 2)
    s = 2 * q - 1

    def chip(step):
        return lax.rem(m + step + 2 * CHIPS, CHIPS)

    def group(step):
        return lax.rem(z + step + 2 * GROUPS, GROUPS)

    sibling = (r - s, z)

    load_z = []
    for half in range(2):
        load_z.append(
            pltpu.make_async_copy(
                z_hbm.at[pl.ds(half * HALF * B, HALF * B)],
                halo.at[OWN, half, pl.ds(0, HALF * B)],
                z_sem.at[half],
            )
        )
        load_z[-1].start()
    load_zcol = pltpu.make_async_copy(zcol_hbm, zcol, small_sem.at[0])
    load_zcol.start()
    load_fcol = pltpu.make_async_copy(fcol_hbm, fcol, small_sem.at[1])
    load_fcol.start()
    load_f = []
    for g in range(4):
        rows = pl.ds(4 * g, 4)
        load_f.append(pltpu.make_async_copy(f_hbm.at[rows], fv.at[rows], f_sem.at[g]))
        load_f[-1].start()

    barrier = pltpu.get_barrier_semaphore()
    peers = [(r, group(1)), (r, group(-1)), sibling, (2 * chip(s) + 1 - q, z)]
    peers += [(2 * chip(j) + q, z) for j in range(1, CHIPS)]
    for peer in peers:
        pl.semaphore_signal(barrier, inc=1, device_id=peer, device_id_type=MESH)

    def remote(src, dst, send, recv, device):
        return pltpu.make_async_remote_copy(
            src_ref=src, dst_ref=dst, send_sem=send, recv_sem=recv,
            device_id=device, device_id_type=MESH,
        )

    sent = []

    def go(copy):
        copy.start()
        sent.append(copy)

    def drain(count):
        for copy in sent[:count]:
            copy.wait_send()
        del sent[:count]

    def ring_copy(sense, distance, half):
        n = group(-sense * (distance - 1))
        at = (0 if sense == 1 else 1, distance - 1, half)
        if distance == 1:
            source = z_hbm.at[pl.ds(half * HALF * B, HALF * B)]
        else:
            source = ring.at[n, half]
        return remote(
            source, ring.at[n, half], ring_send.at[at], ring_recv.at[at], (r, group(sense))
        )

    def ring_wait(sense, distance, half):
        n = group(-sense * distance)
        at = (0 if sense == 1 else 1, distance - 1, half)
        remote(
            ring.at[n, half], ring.at[n, half], ring_send.at[at], ring_recv.at[at],
            (r, group(sense)),
        ).wait_recv()

    def tag_copy(sense, distance):
        n = group(-sense * (distance - 1))
        at = (0 if sense == 1 else 1, distance - 1)
        return remote(
            tags.at[n], tags.at[n], tag_send.at[at], tag_recv.at[at], (r, group(sense))
        )

    def tag_wait(sense, distance):
        n = group(-sense * distance)
        at = (0 if sense == 1 else 1, distance - 1)
        remote(
            tags.at[n], tags.at[n], tag_send.at[at], tag_recv.at[at], (r, group(sense))
        ).wait_recv()

    pl.semaphore_wait(barrier, len(peers))
    go(ring_copy(1, 1, 0))
    go(ring_copy(-1, 1, 1))

    load_zcol.wait()
    load_fcol.wait()
    row_of = lax.broadcasted_iota(jnp.int32, (ROWS, B), 0)

    def mask_tile(first):
        tile = jnp.zeros((ROWS, B), F32)
        for i in range(first, ROWS):
            tile = jnp.where(row_of == i - first, zcol[0, i].astype(F32), tile)
        return tile.astype(BF16)

    tags[z] = mask_tile(0)
    halo[OWN, 0, pl.ds(HALF * B, ROWS)] = mask_tile(0)
    halo[OWN, 1, pl.ds(HALF * B, ROWS)] = mask_tile(HALF)
    for half in range(2):
        load_z[half].wait()

    def halo_copy(step, order, src_slot, dst_slot, device, core=q):
        half = core if order == 0 else 1 - core
        return remote(
            halo.at[src_slot, half], halo.at[dst_slot, half],
            halo_send.at[step, order], halo_recv.at[step, order], device,
        )

    def halo_wait(step, order, slot):
        halo_copy(step, order, slot, slot, sibling, q if step < 2 else 1 - q).wait_recv()

    for order in range(2):
        go(halo_copy(0, order, OWN, 1, (2 * chip(1) + q, z)))
        go(halo_copy(1, order, OWN, 5, (2 * chip(-1) + q, z)))
    for order in range(2):
        go(halo_copy(2, order, OWN, 3 + s, sibling))
    go(ring_copy(1, 1, 1))
    go(ring_copy(-1, 1, 0))
    go(tag_copy(1, 1))
    go(tag_copy(-1, 1))

    def expand_slot(slot, half):
        masks[...] = halo[slot, half, pl.ds(HALF * B, ROWS)].astype(F32)

        @pl.loop(0, HALF)
        def _(j):
            block = halo[slot, half, pl.ds(pl.multiple_of(j * B, B), B)].astype(F32)
            second = masks[pl.ds(j, 1), :]
            at = slot * ROWS + half * HALF + j
            zexp[at, :, 0:B] = (block * (1.0 - second)).astype(BF16)
            zexp[at, :, B:WIDE] = (block * second).astype(BF16)

    def expand_both(slot):
        expand_slot(slot, 0)
        expand_slot(slot, 1)

    expand_both(OWN)
    halo_wait(2, 0, 3 - s)
    halo_wait(2, 1, 3 - s)
    expand_both(3 - s)

    def expand_half(t, half):
        n = group(ORDER[t])
        masks[...] = tags[n].astype(F32)

        @pl.loop(0, HALF)
        def _(j):
            block = ring[n, half, pl.ds(pl.multiple_of(j * B, B), B)].astype(F32)
            second = masks[pl.ds(half * HALF + j, 1), :]
            rows = pl.ds(pl.multiple_of((half * HALF + j) * B, B), B)
            wide[t, rows, 0:B] = (block * (1.0 - second)).astype(BF16)
            wide[t, rows, B:WIDE] = (block * second).astype(BF16)

    def forward(distance, first):
        right, left = (0, 1) if first else (1, 0)
        for sense, half in ((1, right), (-1, left)):
            ring_wait(sense, distance, half)
            if distance < 3 or (distance == 3 and first):
                go(ring_copy(sense, distance + 1, half))
            if first:
                tag_wait(sense, distance)
                if distance < 3 or sense == 1:
                    go(tag_copy(sense, distance + 1))
        expand_half(2 * distance - 1, right)
        expand_half(2 * distance, left)

    def halo_forward(order):
        halo_wait(0, order, 1)
        halo_wait(1, order, 5)
        go(halo_copy(5, order, 3 - 2 * s, 3 - 3 * s, (2 * chip(s) + 1 - q, z)))
        go(halo_copy(3, order, 1, 1 + s, sibling))
        go(halo_copy(4, order, 5, 5 + s, sibling))

    forward(1, True)
    halo_forward(0)
    forward(1, False)
    halo_forward(1)
    expand_both(1)
    expand_both(5)
    for order in range(2):
        halo_wait(3, order, 1 - s)
        halo_wait(4, order, 5 - s)
    expand_both(1 - s)
    expand_both(5 - s)

    first_row = (r - OWN) * ROWS

    def place(column):
        return jnp.minimum(lax.rem(column - first_row + NB, NB), SLOTS * ROWS - 1)

    def product_row(i):
        left = jnp.concatenate([fv[i, pl.ds(k * B, B)] for k in range(K)], axis=1)
        right = jnp.concatenate([zexp[place(fcol[i, k])] for k in range(K)], axis=0)
        acc = jnp.dot(left, right, preferred_element_type=F32)
        rows = pl.ds(pl.multiple_of(i * B, B), B)
        for c in range(CB):
            turned[c * B:(c + 1) * B, rows] = jnp.transpose(acc[:, c * B:(c + 1) * B]).astype(BF16)

    def product_rows(first):
        for i in range(4):
            product_row(first + i)

    for g in range(4):
        load_f[g].wait()
    near = HALF * (1 - q)
    halo_wait(5, 0, 3 + 3 * s)
    expand_slot(3 + 3 * s, 1 - q)
    product_rows(near)
    forward(2, True)
    product_rows(near + 4)
    halo_wait(5, 1, 3 + 3 * s)
    expand_slot(3 + 3 * s, q)
    product_rows(HALF * q)
    forward(2, False)
    product_rows(HALF * q + 4)
    early = len(sent)
    forward(3, True)

    def group_of(t):
        return group(ORDER[t])

    pair_copies = []

    def window(t):
        right = wide[t]
        if t == 0:
            right = zexp[OWN * ROWS:(OWN + 1) * ROWS].reshape(ROWS * B, WIDE)
        product = jnp.transpose(jnp.dot(turned[...], right, preferred_element_type=F32))
        for b in range(4):
            part[t, b % 2, b // 2] = product[b * OUT:(b + 1) * OUT]
        copy = remote(
            part.at[t, 1 - q], other.at[t], pair_send.at[t], pair_recv.at[t], sibling
        )
        pair_copies.append(copy)
        go(copy)

    def sum_copy(t, h):
        d = 2 * group_of(t) + h
        return d, remote(
            chip_sum.at[t, h], arrived.at[m], sum_send.at[t, h], sum_recv.at[m],
            (2 * d + q, z),
        )

    def finish(t):
        pair_copies[t].wait_recv()
        for h in range(2):
            both = part[t, q, h] + other[t, h]
            chip_sum[t, h] = both.astype(BF16)
            d, copy = sum_copy(t, h)

            @pl.when(d == m)
            def _():
                total[...] = both

            @pl.when(d != m)
            def _():
                copy.start()

    window(0)
    window(1)
    window(2)
    finish(0)
    window(3)
    finish(1)
    window(4)
    finish(2)
    forward(3, False)
    window(5)
    finish(3)
    window(6)
    finish(4)
    drain(early)
    tag_wait(1, 4)
    ring_wait(1, 4, 0)
    ring_wait(-1, 4, 1)
    expand_half(7, 0)
    expand_half(7, 1)
    window(7)
    finish(5)
    finish(6)
    finish(7)

    acc = total[...]
    for j in range(1, CHIPS):
        source = chip(j)
        remote(
            arrived.at[source], arrived.at[source], sum_send.at[0, 0], sum_recv.at[source], sibling
        ).wait_recv()
        acc += arrived[source].astype(F32)
    out[...] = acc

    drain(len(sent))
    for t in range(GROUPS):
        for h in range(2):
            d, copy = sum_copy(t, h)

            @pl.when(d != m)
            def _():
                copy.wait_send()


def body(fblocks, fcol, zblocks, zcol):
    dma = pltpu.SemaphoreType.DMA
    return pl.pallas_call(
        kernel,
        out_shape=jax.ShapeDtypeStruct((OUT, WIDE), F32),
        in_specs=[pl.BlockSpec(memory_space=pl.ANY)] * 4,
        out_specs=pl.BlockSpec(memory_space=pltpu.VMEM),
        scratch_shapes=[
            pltpu.VMEM((ROWS, K * B, B), BF16),
            pltpu.VMEM((SLOTS, 2, HALF * B + ROWS, B), BF16),
            pltpu.VMEM((SLOTS * ROWS, B, WIDE), BF16),
            pltpu.VMEM((GROUPS, 2, HALF * B, B), BF16),
            pltpu.VMEM((GROUPS, ROWS, B), BF16),
            pltpu.VMEM((GROUPS, ROWS * B, WIDE), BF16),
            pltpu.VMEM((WIDE, ROWS * B), BF16),
            pltpu.VMEM((ROWS, B), F32),
            pltpu.VMEM((GROUPS, 2, 2, OUT, WIDE), F32),
            pltpu.VMEM((GROUPS, 2, OUT, WIDE), F32),
            pltpu.VMEM((GROUPS, 2, OUT, WIDE), BF16),
            pltpu.VMEM((CHIPS, OUT, WIDE), BF16),
            pltpu.VMEM((OUT, WIDE), F32),
            pltpu.SMEM((ROWS, K), jnp.int32),
            pltpu.SMEM((1, ROWS), jnp.int32),
            dma((2,)),
            dma((2,)),
            dma((4,)),
            dma((6, 2)),
            dma((6, 2)),
            dma((2, 4, 2)),
            dma((2, 4, 2)),
            dma((2, 4)),
            dma((2, 4)),
            dma((GROUPS,)),
            dma((GROUPS,)),
            dma((GROUPS, 2)),
            dma((CHIPS,)),
        ],
        compiler_params=pltpu.CompilerParams(
            collective_id=0, has_side_effects=True, vmem_limit_bytes=60 * 2**20
        ),
    )(
        fcol,
        zcol.reshape(1, ROWS),
        fblocks.reshape(ROWS, K * B, B),
        zblocks.reshape(ROWS * B, B),
    )


def solution(mesh):
    in_specs = (
        P("rows", None, None, None),
        P("rows", None),
        P("rows", "cols", None, None),
        P("rows", "cols"),
    )
    out_specs = P("rows", "cols")
    return jax.shard_map(body, mesh=mesh, in_specs=in_specs, out_specs=out_specs, check_vma=False)
```

```python
import jax
import jax.numpy as jnp
from jax import lax
from jax.experimental import pallas as pl
from jax.experimental.pallas import tpu as pltpu
from jax.sharding import PartitionSpec as P

B = 128
K = 20
CB = 2
ROWS = 16
CHIPS = 16
GROUPS = 8
NB = 512
SLOTS = 7
OWN = 3
HALF = ROWS // 2
WIDE = CB * B
OUT = 64
SUB = 4
LAST = GROUPS - 1
ORDER = (0, -1, 1, -2, 2, -3, 3, 4)
MESH = pl.DeviceIdType.MESH
F32 = jnp.float32
BF16 = jnp.bfloat16


def kernel(
    fcol_hbm,
    zcol_hbm,
    f_hbm,
    z_hbm,
    out,
    fv,
    halo,
    zexp,
    ring,
    tags,
    wide,
    turned,
    masks,
    part,
    other,
    chip_sum,
    arrived,
    total,
    fcol,
    zcol,
    small_sem,
    z_sem,
    f_sem,
    halo_send,
    halo_recv,
    ring_send,
    ring_recv,
    tag_send,
    tag_recv,
    pair_send,
    pair_recv,
    sum_send,
    sum_recv,
    last_send,
    last_recv,
):
    r = lax.axis_index("rows")
    z = lax.axis_index("cols")
    m = lax.div(r, 2)
    q = lax.rem(r, 2)
    s = 2 * q - 1

    def chip(step):
        return lax.rem(m + step + 2 * CHIPS, CHIPS)

    def group(step):
        return lax.rem(z + step + 2 * GROUPS, GROUPS)

    sibling = (r - s, z)

    load_z = []
    for half in range(2):
        load_z.append(
            pltpu.make_async_copy(
                z_hbm.at[pl.ds(half * HALF * B, HALF * B)],
                halo.at[OWN, half, pl.ds(0, HALF * B)],
                z_sem.at[half],
            )
        )
        load_z[-1].start()
    load_zcol = pltpu.make_async_copy(zcol_hbm, zcol, small_sem.at[0])
    load_zcol.start()
    load_fcol = pltpu.make_async_copy(fcol_hbm, fcol, small_sem.at[1])
    load_fcol.start()
    load_f = []
    for g in range(4):
        rows = pl.ds(4 * g, 4)
        load_f.append(pltpu.make_async_copy(f_hbm.at[rows], fv.at[rows], f_sem.at[g]))
        load_f[-1].start()

    barrier = pltpu.get_barrier_semaphore()
    peers = [(r, group(1)), (r, group(-1)), sibling, (2 * chip(s) + 1 - q, z)]
    peers += [(2 * chip(j) + q, z) for j in range(1, CHIPS)]
    for peer in peers:
        pl.semaphore_signal(barrier, inc=1, device_id=peer, device_id_type=MESH)

    def remote(src, dst, send, recv, device):
        return pltpu.make_async_remote_copy(
            src_ref=src, dst_ref=dst, send_sem=send, recv_sem=recv,
            device_id=device, device_id_type=MESH,
        )

    sent = []

    def go(copy):
        copy.start()
        sent.append(copy)

    def drain(count):
        for copy in sent[:count]:
            copy.wait_send()
        del sent[:count]

    def ring_copy(sense, distance, half):
        n = group(-sense * (distance - 1))
        at = (0 if sense == 1 else 1, distance - 1, half)
        if distance == 1:
            source = z_hbm.at[pl.ds(half * HALF * B, HALF * B)]
        else:
            source = ring.at[n, half]
        return remote(
            source, ring.at[n, half], ring_send.at[at], ring_recv.at[at], (r, group(sense))
        )

    def ring_wait(sense, distance, half):
        n = group(-sense * distance)
        at = (0 if sense == 1 else 1, distance - 1, half)
        remote(
            ring.at[n, half], ring.at[n, half], ring_send.at[at], ring_recv.at[at],
            (r, group(sense)),
        ).wait_recv()

    def last_copy(sense, sub, distance=3):
        n = group(-sense * distance)
        half = 0 if sense == 1 else 1
        at = (half, sub)
        part_of = ring.at[n, half, pl.ds(sub * SUB * B, SUB * B)]
        return remote(part_of, part_of, last_send.at[at], last_recv.at[at], (r, group(sense)))

    def last_wait(sense, sub):
        last_copy(sense, sub, 4).wait_recv()

    def tag_copy(sense, distance):
        n = group(-sense * (distance - 1))
        at = (0 if sense == 1 else 1, distance - 1)
        return remote(
            tags.at[n], tags.at[n], tag_send.at[at], tag_recv.at[at], (r, group(sense))
        )

    def tag_wait(sense, distance):
        n = group(-sense * distance)
        at = (0 if sense == 1 else 1, distance - 1)
        remote(
            tags.at[n], tags.at[n], tag_send.at[at], tag_recv.at[at], (r, group(sense))
        ).wait_recv()

    pl.semaphore_wait(barrier, len(peers))
    go(ring_copy(1, 1, 0))
    go(ring_copy(-1, 1, 1))

    load_zcol.wait()
    load_fcol.wait()
    row_of = lax.broadcasted_iota(jnp.int32, (ROWS, B), 0)

    def mask_tile(first):
        tile = jnp.zeros((ROWS, B), F32)
        for i in range(first, ROWS):
            tile = jnp.where(row_of == i - first, zcol[0, i].astype(F32), tile)
        return tile.astype(BF16)

    tags[z] = mask_tile(0)
    halo[OWN, 0, pl.ds(HALF * B, ROWS)] = mask_tile(0)
    halo[OWN, 1, pl.ds(HALF * B, ROWS)] = mask_tile(HALF)
    for half in range(2):
        load_z[half].wait()

    def halo_copy(step, order, src_slot, dst_slot, device, core=q):
        half = core if order == 0 else 1 - core
        return remote(
            halo.at[src_slot, half], halo.at[dst_slot, half],
            halo_send.at[step, order], halo_recv.at[step, order], device,
        )

    def halo_wait(step, order, slot):
        halo_copy(step, order, slot, slot, sibling, q if step < 2 else 1 - q).wait_recv()

    for order in range(2):
        go(halo_copy(0, order, OWN, 1, (2 * chip(1) + q, z)))
        go(halo_copy(1, order, OWN, 5, (2 * chip(-1) + q, z)))
    for order in range(2):
        go(halo_copy(2, order, OWN, 3 + s, sibling))
    go(ring_copy(1, 1, 1))
    go(ring_copy(-1, 1, 0))
    go(tag_copy(1, 1))
    go(tag_copy(-1, 1))

    def expand_slot(slot, half):
        masks[...] = halo[slot, half, pl.ds(HALF * B, ROWS)].astype(F32)

        @pl.loop(0, HALF)
        def _(j):
            block = halo[slot, half, pl.ds(pl.multiple_of(j * B, B), B)]
            second = masks[pl.ds(j, 1), :].astype(BF16)
            at = slot * ROWS + half * HALF + j
            zexp[at, :, 0:B] = block * (1 - second)
            zexp[at, :, B:WIDE] = block * second

    def expand_both(slot):
        expand_slot(slot, 0)
        expand_slot(slot, 1)

    expand_both(OWN)
    halo_wait(2, 0, 3 - s)
    halo_wait(2, 1, 3 - s)
    expand_both(3 - s)

    def expand_half(t, half, first=0, last=HALF):
        n = group(ORDER[t])
        masks[...] = tags[n].astype(F32)

        @pl.loop(first, last)
        def _(j):
            block = ring[n, half, pl.ds(pl.multiple_of(j * B, B), B)]
            second = masks[pl.ds(half * HALF + j, 1), :].astype(BF16)
            rows = pl.ds(pl.multiple_of((half * HALF + j) * B, B), B)
            wide[t, rows, 0:B] = block * (1 - second)
            wide[t, rows, B:WIDE] = block * second

    def forward(distance, first):
        right, left = (0, 1) if first else (1, 0)
        for sense, half in ((1, right), (-1, left)):
            ring_wait(sense, distance, half)
            if distance < 3:
                go(ring_copy(sense, distance + 1, half))
            elif first:
                for sub in range(2):
                    go(last_copy(sense, sub))
            if first:
                tag_wait(sense, distance)
                if distance < 3 or sense == 1:
                    go(tag_copy(sense, distance + 1))
        expand_half(2 * distance - 1, right)
        expand_half(2 * distance, left)

    def halo_forward(order):
        halo_wait(0, order, 1)
        halo_wait(1, order, 5)
        go(halo_copy(5, order, 3 - 2 * s, 3 - 3 * s, (2 * chip(s) + 1 - q, z)))
        go(halo_copy(3, order, 1, 1 + s, sibling))
        go(halo_copy(4, order, 5, 5 + s, sibling))

    forward(1, True)
    halo_forward(0)
    forward(1, False)
    halo_forward(1)
    expand_both(1)
    expand_both(5)
    for order in range(2):
        halo_wait(3, order, 1 - s)
        halo_wait(4, order, 5 - s)
    expand_both(1 - s)
    expand_both(5 - s)

    first_row = (r - OWN) * ROWS

    def place(column):
        return jnp.minimum(lax.rem(column - first_row + NB, NB), SLOTS * ROWS - 1)

    def product_row(i):
        left = jnp.concatenate([fv[i, pl.ds(k * B, B)] for k in range(K)], axis=1)
        right = jnp.concatenate([zexp[place(fcol[i, k])] for k in range(K)], axis=0)
        acc = jnp.dot(left, right, preferred_element_type=F32)
        rows = pl.ds(pl.multiple_of(i * B, B), B)
        for c in range(CB):
            turned[c * B:(c + 1) * B, rows] = jnp.transpose(acc[:, c * B:(c + 1) * B].astype(BF16))

    def product_rows(first):
        for i in range(4):
            product_row(first + i)

    for g in range(4):
        load_f[g].wait()
    near = HALF * (1 - q)
    halo_wait(5, 0, 3 + 3 * s)
    expand_slot(3 + 3 * s, 1 - q)
    product_rows(near)
    forward(2, True)
    product_rows(near + 4)
    halo_wait(5, 1, 3 + 3 * s)
    expand_slot(3 + 3 * s, q)
    product_rows(HALF * q)
    forward(2, False)
    product_rows(HALF * q + 4)

    def group_of(t):
        return group(ORDER[t])

    pair_copies = []

    def last_product():
        acc = jnp.zeros((WIDE, WIDE), F32)
        for sub in range(2):
            for sense, half in ((1, 0), (-1, 1)):
                last_wait(sense, sub)
                expand_half(LAST, half, sub * SUB, (sub + 1) * SUB)
                rows = pl.ds((half * HALF + sub * SUB) * B, SUB * B)
                acc += jnp.dot(turned[:, rows], wide[LAST, rows], preferred_element_type=F32)
        return acc

    def window(t):
        if t == LAST:
            product = last_product()
        else:
            right = wide[t]
            if t == 0:
                right = zexp[OWN * ROWS:(OWN + 1) * ROWS].reshape(ROWS * B, WIDE)
            product = jnp.dot(turned[...], right, preferred_element_type=F32)
        product = jnp.transpose(product)
        for b in range(4):
            part[t, b % 2, b // 2] = product[b * OUT:(b + 1) * OUT]
        copy = remote(
            part.at[t, 1 - q], other.at[t], pair_send.at[t], pair_recv.at[t], sibling
        )
        pair_copies.append(copy)
        go(copy)

    def sum_copy(t, h):
        d = 2 * group_of(t) + h
        return d, remote(
            chip_sum.at[t, h], arrived.at[m], sum_send.at[t, h], sum_recv.at[m],
            (2 * d + q, z),
        )

    def finish(t):
        pair_copies[t].wait_recv()
        for h in range(2):
            both = part[t, q, h] + other[t, h]
            chip_sum[t, h] = both.astype(BF16)
            d, copy = sum_copy(t, h)

            @pl.when(d == m)
            def _():
                total[...] = both

            @pl.when(d != m)
            def _():
                copy.start()

    window(0)
    early = len(sent)
    forward(3, True)
    window(1)
    finish(0)
    window(2)
    finish(1)
    window(3)
    finish(2)
    window(4)
    finish(3)
    finish(4)
    forward(3, False)
    window(5)
    window(6)
    finish(5)
    finish(6)
    drain(early)
    tag_wait(1, 4)
    window(7)
    finish(7)

    acc = total[...]
    for j in range(1, CHIPS):
        source = chip(j)
        remote(
            arrived.at[source], arrived.at[source], sum_send.at[0, 0], sum_recv.at[source], sibling
        ).wait_recv()
        acc += arrived[source].astype(F32)
    out[...] = acc

    drain(len(sent))
    for t in range(GROUPS):
        for h in range(2):
            d, copy = sum_copy(t, h)

            @pl.when(d != m)
            def _():
                copy.wait_send()


def body(fblocks, fcol, zblocks, zcol):
    dma = pltpu.SemaphoreType.DMA
    return pl.pallas_call(
        kernel,
        out_shape=jax.ShapeDtypeStruct((OUT, WIDE), F32),
        in_specs=[pl.BlockSpec(memory_space=pl.ANY)] * 4,
        out_specs=pl.BlockSpec(memory_space=pltpu.VMEM),
        scratch_shapes=[
            pltpu.VMEM((ROWS, K * B, B), BF16),
            pltpu.VMEM((SLOTS, 2, HALF * B + ROWS, B), BF16),
            pltpu.VMEM((SLOTS * ROWS, B, WIDE), BF16),
            pltpu.VMEM((GROUPS, 2, HALF * B, B), BF16),
            pltpu.VMEM((GROUPS, ROWS, B), BF16),
            pltpu.VMEM((GROUPS, ROWS * B, WIDE), BF16),
            pltpu.VMEM((WIDE, ROWS * B), BF16),
            pltpu.VMEM((ROWS, B), F32),
            pltpu.VMEM((GROUPS, 2, 2, OUT, WIDE), F32),
            pltpu.VMEM((GROUPS, 2, OUT, WIDE), F32),
            pltpu.VMEM((GROUPS, 2, OUT, WIDE), BF16),
            pltpu.VMEM((CHIPS, OUT, WIDE), BF16),
            pltpu.VMEM((OUT, WIDE), F32),
            pltpu.SMEM((ROWS, K), jnp.int32),
            pltpu.SMEM((1, ROWS), jnp.int32),
            dma((2,)),
            dma((2,)),
            dma((4,)),
            dma((6, 2)),
            dma((6, 2)),
            dma((2, 4, 2)),
            dma((2, 4, 2)),
            dma((2, 4)),
            dma((2, 4)),
            dma((GROUPS,)),
            dma((GROUPS,)),
            dma((GROUPS, 2)),
            dma((CHIPS,)),
            dma((2, 2)),
            dma((2, 2)),
        ],
        compiler_params=pltpu.CompilerParams(
            collective_id=0, has_side_effects=True, vmem_limit_bytes=60 * 2**20
        ),
    )(
        fcol,
        zcol.reshape(1, ROWS),
        fblocks.reshape(ROWS, K * B, B),
        zblocks.reshape(ROWS * B, B),
    )


def solution(mesh):
    in_specs = (
        P("rows", None, None, None),
        P("rows", None),
        P("rows", "cols", None, None),
        P("rows", "cols"),
    )
    out_specs = P("rows", "cols")
    return jax.shard_map(body, mesh=mesh, in_specs=in_specs, out_specs=out_specs, check_vma=False)
```

```python
import jax
import jax.numpy as jnp
from jax import lax
from jax.experimental import pallas as pl
from jax.experimental.pallas import tpu as pltpu
from jax.sharding import PartitionSpec as P

B = 128
K = 20
CB = 2
ROWS = 16
CHIPS = 16
GROUPS = 8
NB = 512
SLOTS = 7
OWN = 3
HALF = ROWS // 2
WIDE = CB * B
OUT = 64
SUB = 4
LAST = GROUPS - 1
ORDER = (0, -1, 1, -2, 2, -3, 3, 4)
MESH = pl.DeviceIdType.MESH
F32 = jnp.float32
BF16 = jnp.bfloat16


def kernel(
    fcol_hbm,
    zcol_hbm,
    f_hbm,
    z_hbm,
    out,
    fv,
    halo,
    zexp,
    ring,
    tags,
    wide,
    turned,
    masks,
    part,
    other,
    chip_sum,
    arrived,
    total,
    fcol,
    zcol,
    small_sem,
    z_sem,
    f_sem,
    halo_send,
    halo_recv,
    ring_send,
    ring_recv,
    tag_send,
    tag_recv,
    pair_send,
    pair_recv,
    sum_send,
    sum_recv,
    last_send,
    last_recv,
):
    r = lax.axis_index("rows")
    z = lax.axis_index("cols")
    m = lax.div(r, 2)
    q = lax.rem(r, 2)
    s = 2 * q - 1

    def chip(step):
        return lax.rem(m + step + 2 * CHIPS, CHIPS)

    def group(step):
        return lax.rem(z + step + 2 * GROUPS, GROUPS)

    sibling = (r - s, z)

    load_z = []
    for half in range(2):
        load_z.append(
            pltpu.make_async_copy(
                z_hbm.at[pl.ds(half * HALF * B, HALF * B)],
                halo.at[OWN, half, pl.ds(0, HALF * B)],
                z_sem.at[half],
            )
        )
        load_z[-1].start()
    load_zcol = pltpu.make_async_copy(zcol_hbm, zcol, small_sem.at[0])
    load_zcol.start()
    load_fcol = pltpu.make_async_copy(fcol_hbm, fcol, small_sem.at[1])
    load_fcol.start()
    load_f = []
    for g in range(4):
        rows = pl.ds(4 * g, 4)
        load_f.append(pltpu.make_async_copy(f_hbm.at[rows], fv.at[rows], f_sem.at[g]))
        load_f[-1].start()

    barrier = pltpu.get_barrier_semaphore()
    peers = [(r, group(1)), (r, group(-1)), sibling, (2 * chip(s) + 1 - q, z)]
    peers += [(2 * chip(j) + q, z) for j in range(1, CHIPS)]
    for peer in peers:
        pl.semaphore_signal(barrier, inc=1, device_id=peer, device_id_type=MESH)

    def remote(src, dst, send, recv, device):
        return pltpu.make_async_remote_copy(
            src_ref=src, dst_ref=dst, send_sem=send, recv_sem=recv,
            device_id=device, device_id_type=MESH,
        )

    sent = []

    def go(copy):
        copy.start()
        sent.append(copy)

    def drain(count):
        for copy in sent[:count]:
            copy.wait_send()
        del sent[:count]

    def ring_copy(sense, distance, half):
        n = group(-sense * (distance - 1))
        at = (0 if sense == 1 else 1, distance - 1, half)
        if distance == 1:
            source = z_hbm.at[pl.ds(half * HALF * B, HALF * B)]
        else:
            source = ring.at[n, half]
        return remote(
            source, ring.at[n, half], ring_send.at[at], ring_recv.at[at], (r, group(sense))
        )

    def ring_wait(sense, distance, half):
        n = group(-sense * distance)
        at = (0 if sense == 1 else 1, distance - 1, half)
        remote(
            ring.at[n, half], ring.at[n, half], ring_send.at[at], ring_recv.at[at],
            (r, group(sense)),
        ).wait_recv()

    def last_copy(sense, sub, distance=3):
        n = group(-sense * distance)
        half = 0 if sense == 1 else 1
        at = (half, sub)
        part_of = ring.at[n, half, pl.ds(sub * SUB * B, SUB * B)]
        return remote(part_of, part_of, last_send.at[at], last_recv.at[at], (r, group(sense)))

    def last_wait(sense, sub):
        last_copy(sense, sub, 4).wait_recv()

    def tag_copy(sense, distance):
        n = group(-sense * (distance - 1))
        at = (0 if sense == 1 else 1, distance - 1)
        return remote(
            tags.at[n], tags.at[n], tag_send.at[at], tag_recv.at[at], (r, group(sense))
        )

    def tag_wait(sense, distance):
        n = group(-sense * distance)
        at = (0 if sense == 1 else 1, distance - 1)
        remote(
            tags.at[n], tags.at[n], tag_send.at[at], tag_recv.at[at], (r, group(sense))
        ).wait_recv()

    pl.semaphore_wait(barrier, len(peers))
    go(ring_copy(1, 1, 0))
    go(ring_copy(-1, 1, 1))

    load_zcol.wait()
    load_fcol.wait()
    row_of = lax.broadcasted_iota(jnp.int32, (ROWS, B), 0)

    def mask_tile(first):
        tile = jnp.zeros((ROWS, B), F32)
        for i in range(first, ROWS):
            tile = jnp.where(row_of == i - first, zcol[0, i].astype(F32), tile)
        return tile.astype(BF16)

    tags[z] = mask_tile(0)
    halo[OWN, 0, pl.ds(HALF * B, ROWS)] = mask_tile(0)
    halo[OWN, 1, pl.ds(HALF * B, ROWS)] = mask_tile(HALF)
    for half in range(2):
        load_z[half].wait()

    def halo_copy(step, order, src_slot, dst_slot, device, core=q):
        half = core if order == 0 else 1 - core
        return remote(
            halo.at[src_slot, half], halo.at[dst_slot, half],
            halo_send.at[step, order], halo_recv.at[step, order], device,
        )

    def halo_wait(step, order, slot):
        halo_copy(step, order, slot, slot, sibling, q if step < 2 else 1 - q).wait_recv()

    for order in range(2):
        go(halo_copy(0, order, OWN, 1, (2 * chip(1) + q, z)))
        go(halo_copy(1, order, OWN, 5, (2 * chip(-1) + q, z)))
    for order in range(2):
        go(halo_copy(2, order, OWN, 3 + s, sibling))
    go(ring_copy(1, 1, 1))
    go(ring_copy(-1, 1, 0))
    go(tag_copy(1, 1))
    go(tag_copy(-1, 1))

    def expand_slot(slot, half):
        masks[...] = halo[slot, half, pl.ds(HALF * B, ROWS)].astype(F32)

        @pl.loop(0, HALF)
        def _(j):
            block = halo[slot, half, pl.ds(pl.multiple_of(j * B, B), B)]
            second = masks[pl.ds(j, 1), :].astype(BF16)
            at = slot * ROWS + half * HALF + j
            zexp[at, :, 0:B] = block * (1 - second)
            zexp[at, :, B:WIDE] = block * second

    def expand_both(slot):
        expand_slot(slot, 0)
        expand_slot(slot, 1)

    expand_both(OWN)
    halo_wait(2, 0, 3 - s)
    halo_wait(2, 1, 3 - s)
    expand_both(3 - s)

    def expand_half(t, half, first=0, last=HALF):
        n = group(ORDER[t])
        masks[...] = tags[n].astype(F32)

        @pl.loop(first, last)
        def _(j):
            block = ring[n, half, pl.ds(pl.multiple_of(j * B, B), B)]
            second = masks[pl.ds(half * HALF + j, 1), :].astype(BF16)
            rows = pl.ds(pl.multiple_of((half * HALF + j) * B, B), B)
            wide[t, rows, 0:B] = block * (1 - second)
            wide[t, rows, B:WIDE] = block * second

    def forward(distance, first):
        right, left = (0, 1) if first else (1, 0)
        for sense, half in ((1, right), (-1, left)):
            ring_wait(sense, distance, half)
            if distance < 3:
                go(ring_copy(sense, distance + 1, half))
            elif first:
                for sub in range(2):
                    go(last_copy(sense, sub))
            if first:
                tag_wait(sense, distance)
                if distance < 3 or sense == 1:
                    go(tag_copy(sense, distance + 1))
        expand_half(2 * distance - 1, right)
        expand_half(2 * distance, left)

    def halo_forward(order):
        halo_wait(0, order, 1)
        halo_wait(1, order, 5)
        go(halo_copy(5, order, 3 - 2 * s, 3 - 3 * s, (2 * chip(s) + 1 - q, z)))
        go(halo_copy(3, order, 1, 1 + s, sibling))
        go(halo_copy(4, order, 5, 5 + s, sibling))

    forward(1, True)
    halo_forward(0)
    forward(1, False)
    halo_forward(1)
    expand_both(1)
    expand_both(5)
    for order in range(2):
        halo_wait(3, order, 1 - s)
        halo_wait(4, order, 5 - s)
    expand_both(1 - s)
    expand_both(5 - s)

    first_row = (r - OWN) * ROWS

    def place(column):
        return jnp.minimum(lax.rem(column - first_row + NB, NB), SLOTS * ROWS - 1)

    def product_row(i):
        left = jnp.concatenate([fv[i, pl.ds(k * B, B)] for k in range(K)], axis=1)
        right = jnp.concatenate([zexp[place(fcol[i, k])] for k in range(K)], axis=0)
        acc = jnp.dot(left, right, preferred_element_type=F32)
        rows = pl.ds(pl.multiple_of(i * B, B), B)
        for c in range(CB):
            turned[c * B:(c + 1) * B, rows] = jnp.transpose(acc[:, c * B:(c + 1) * B].astype(BF16))

    def product_rows(first):
        for i in range(4):
            product_row(first + i)

    for g in range(4):
        load_f[g].wait()
    near = HALF * (1 - q)
    halo_wait(5, 0, 3 + 3 * s)
    expand_slot(3 + 3 * s, 1 - q)
    product_rows(near)
    forward(2, True)
    product_rows(near + 4)
    halo_wait(5, 1, 3 + 3 * s)
    expand_slot(3 + 3 * s, q)
    product_rows(HALF * q)
    forward(2, False)
    product_rows(HALF * q + 4)

    def group_of(t):
        return group(ORDER[t])

    pair_copies = []

    def last_product():
        acc = jnp.zeros((WIDE, WIDE), F32)
        for sub in range(2):
            for sense, half in ((1, 0), (-1, 1)):
                last_wait(sense, sub)
                expand_half(LAST, half, sub * SUB, (sub + 1) * SUB)
                rows = pl.ds((half * HALF + sub * SUB) * B, SUB * B)
                acc += jnp.dot(turned[:, rows], wide[LAST, rows], preferred_element_type=F32)
        return acc

    def window(t):
        if t == LAST:
            product = last_product()
        else:
            right = wide[t]
            if t == 0:
                right = zexp[OWN * ROWS:(OWN + 1) * ROWS].reshape(ROWS * B, WIDE)
            product = jnp.dot(turned[...], right, preferred_element_type=F32)
        product = jnp.transpose(product)
        for b in range(4):
            part[t, b % 2, b // 2] = product[b * OUT:(b + 1) * OUT]
        copy = remote(
            part.at[t, 1 - q], other.at[t], pair_send.at[t], pair_recv.at[t], sibling
        )
        pair_copies.append(copy)
        go(copy)

    def sum_copy(t, h):
        d = 2 * group_of(t) + h
        return d, remote(
            chip_sum.at[t, h], arrived.at[m], sum_send.at[t, h], sum_recv.at[m],
            (2 * d + q, z),
        )

    def finish(t):
        pair_copies[t].wait_recv()
        for h in range(2):
            both = part[t, q, h] + other[t, h]
            chip_sum[t, h] = both.astype(BF16)
            d, copy = sum_copy(t, h)

            @pl.when(d == m)
            def _():
                total[...] = both

            @pl.when(d != m)
            def _():
                copy.start()

    window(0)
    early = len(sent)
    forward(3, True)
    window(1)
    finish(0)
    window(2)
    finish(1)
    window(3)
    finish(2)
    window(4)
    finish(3)
    finish(4)
    forward(3, False)
    window(5)
    window(6)
    finish(5)
    finish(6)
    drain(early)
    tag_wait(1, 4)
    window(7)
    finish(7)

    acc = total[...]
    for j in range(1, CHIPS):
        source = chip(j)
        remote(
            arrived.at[source], arrived.at[source], sum_send.at[0, 0], sum_recv.at[source], sibling
        ).wait_recv()
        acc += arrived[source].astype(F32)
    out[...] = acc

    drain(len(sent))
    for t in range(GROUPS):
        for h in range(2):
            d, copy = sum_copy(t, h)

            @pl.when(d != m)
            def _():
                copy.wait_send()


def body(fblocks, fcol, zblocks, zcol):
    dma = pltpu.SemaphoreType.DMA
    return pl.pallas_call(
        kernel,
        out_shape=pltpu.VMEM((OUT, WIDE), F32),
        in_specs=[pl.BlockSpec(memory_space=pl.ANY)] * 4,
        out_specs=pl.BlockSpec(memory_space=pltpu.VMEM),
        scratch_shapes=[
            pltpu.VMEM((ROWS, K * B, B), BF16),
            pltpu.VMEM((SLOTS, 2, HALF * B + ROWS, B), BF16),
            pltpu.VMEM((SLOTS * ROWS, B, WIDE), BF16),
            pltpu.VMEM((GROUPS, 2, HALF * B, B), BF16),
            pltpu.VMEM((GROUPS, ROWS, B), BF16),
            pltpu.VMEM((GROUPS, ROWS * B, WIDE), BF16),
            pltpu.VMEM((WIDE, ROWS * B), BF16),
            pltpu.VMEM((ROWS, B), F32),
            pltpu.VMEM((GROUPS, 2, 2, OUT, WIDE), F32),
            pltpu.VMEM((GROUPS, 2, OUT, WIDE), F32),
            pltpu.VMEM((GROUPS, 2, OUT, WIDE), BF16),
            pltpu.VMEM((CHIPS, OUT, WIDE), BF16),
            pltpu.VMEM((OUT, WIDE), F32),
            pltpu.SMEM((ROWS, K), jnp.int32),
            pltpu.SMEM((1, ROWS), jnp.int32),
            dma((2,)),
            dma((2,)),
            dma((4,)),
            dma((6, 2)),
            dma((6, 2)),
            dma((2, 4, 2)),
            dma((2, 4, 2)),
            dma((2, 4)),
            dma((2, 4)),
            dma((GROUPS,)),
            dma((GROUPS,)),
            dma((GROUPS, 2)),
            dma((CHIPS,)),
            dma((2, 2)),
            dma((2, 2)),
        ],
        compiler_params=pltpu.CompilerParams(
            collective_id=0, has_side_effects=True, vmem_limit_bytes=60 * 2**20
        ),
    )(
        fcol,
        zcol.reshape(1, ROWS),
        fblocks.reshape(ROWS, K * B, B),
        zblocks.reshape(ROWS * B, B),
    )


def solution(mesh):
    in_specs = (
        P("rows", None, None, None),
        P("rows", None),
        P("rows", "cols", None, None),
        P("rows", "cols"),
    )
    out_specs = P("rows", "cols")
    return jax.shard_map(body, mesh=mesh, in_specs=in_specs, out_specs=out_specs, check_vma=False)
```

```python
import jax
import jax.numpy as jnp
from jax import lax
from jax.experimental import pallas as pl
from jax.experimental.pallas import tpu as pltpu
from jax.sharding import PartitionSpec as P

B = 128
K = 20
CB = 2
ROWS = 16
CHIPS = 16
GROUPS = 8
NB = 512
SLOTS = 7
OWN = 3
HALF = ROWS // 2
WIDE = CB * B
OUT = 64
CHUNKS = 4
CHUNK = ROWS // CHUNKS
LAST = GROUPS - 1
ORDER = (0, -1, 1, -2, 2, -3, 3, 4)
MESH = pl.DeviceIdType.MESH
F32 = jnp.float32
BF16 = jnp.bfloat16


def kernel(
    fcol_hbm,
    zcol_hbm,
    f_hbm,
    z_hbm,
    out,
    fv,
    halo,
    zexp,
    ring,
    tags,
    wide,
    turned,
    masks,
    part,
    other,
    chip_sum,
    arrived,
    total,
    fcol,
    zcol,
    small_sem,
    z_sem,
    f_sem,
    halo_send,
    halo_recv,
    ring_send,
    ring_recv,
    tag_send,
    tag_recv,
    pair_send,
    pair_recv,
    sum_send,
    sum_recv,
):
    r = lax.axis_index("rows")
    z = lax.axis_index("cols")
    m = lax.div(r, 2)
    q = lax.rem(r, 2)
    s = 2 * q - 1

    def chip(step):
        return lax.rem(m + step + 2 * CHIPS, CHIPS)

    def group(step):
        return lax.rem(z + step + 2 * GROUPS, GROUPS)

    sibling = (r - s, z)

    load_z = []
    for half in range(2):
        load_z.append(
            pltpu.make_async_copy(
                z_hbm.at[pl.ds(half * HALF * B, HALF * B)],
                halo.at[OWN, half, pl.ds(0, HALF * B)],
                z_sem.at[half],
            )
        )
        load_z[-1].start()
    load_zcol = pltpu.make_async_copy(zcol_hbm, zcol, small_sem.at[0])
    load_zcol.start()
    load_fcol = pltpu.make_async_copy(fcol_hbm, fcol, small_sem.at[1])
    load_fcol.start()
    load_f = []
    for g in range(4):
        rows = pl.ds(4 * g, 4)
        load_f.append(pltpu.make_async_copy(f_hbm.at[rows], fv.at[rows], f_sem.at[g]))
        load_f[-1].start()

    barrier = pltpu.get_barrier_semaphore()
    peers = [(r, group(1)), (r, group(-1)), sibling, (2 * chip(s) + 1 - q, z)]
    peers += [(2 * chip(j) + q, z) for j in range(1, CHIPS)]
    for peer in peers:
        pl.semaphore_signal(barrier, inc=1, device_id=peer, device_id_type=MESH)

    def remote(src, dst, send, recv, device):
        return pltpu.make_async_remote_copy(
            src_ref=src, dst_ref=dst, send_sem=send, recv_sem=recv,
            device_id=device, device_id_type=MESH,
        )

    sent = []

    def go(copy):
        copy.start()
        sent.append(copy)

    def drain(count):
        for copy in sent[:count]:
            copy.wait_send()
        del sent[:count]

    def ring_copy(sense, distance, chunk):
        n = group(-sense * (distance - 1))
        at = (0 if sense == 1 else 1, distance - 1, chunk)
        if distance == 1:
            source = z_hbm.at[pl.ds(chunk * CHUNK * B, CHUNK * B)]
        else:
            source = ring.at[n, chunk]
        return remote(
            source, ring.at[n, chunk], ring_send.at[at], ring_recv.at[at], (r, group(sense))
        )

    def ring_wait(sense, distance, chunk):
        n = group(-sense * distance)
        at = (0 if sense == 1 else 1, distance - 1, chunk)
        remote(
            ring.at[n, chunk], ring.at[n, chunk], ring_send.at[at], ring_recv.at[at],
            (r, group(sense)),
        ).wait_recv()

    def tag_copy(sense, distance):
        n = group(-sense * (distance - 1))
        at = (0 if sense == 1 else 1, distance - 1)
        return remote(
            tags.at[n], tags.at[n], tag_send.at[at], tag_recv.at[at], (r, group(sense))
        )

    def tag_wait(sense, distance):
        n = group(-sense * distance)
        at = (0 if sense == 1 else 1, distance - 1)
        remote(
            tags.at[n], tags.at[n], tag_send.at[at], tag_recv.at[at], (r, group(sense))
        ).wait_recv()

    pl.semaphore_wait(barrier, len(peers))
    go(ring_copy(1, 1, 0))
    go(ring_copy(-1, 1, CHUNKS - 1))

    load_zcol.wait()
    load_fcol.wait()
    row_of = lax.broadcasted_iota(jnp.int32, (ROWS, B), 0)

    def mask_tile(first):
        tile = jnp.zeros((ROWS, B), F32)
        for i in range(first, ROWS):
            tile = jnp.where(row_of == i - first, zcol[0, i].astype(F32), tile)
        return tile.astype(BF16)

    tags[z] = mask_tile(0)
    go(tag_copy(1, 1))
    go(tag_copy(-1, 1))
    halo[OWN, 0, pl.ds(HALF * B, ROWS)] = mask_tile(0)
    halo[OWN, 1, pl.ds(HALF * B, ROWS)] = mask_tile(HALF)
    for half in range(2):
        load_z[half].wait()

    def halo_copy(step, order, src_slot, dst_slot, device, core=q):
        half = core if order == 0 else 1 - core
        return remote(
            halo.at[src_slot, half], halo.at[dst_slot, half],
            halo_send.at[step, order], halo_recv.at[step, order], device,
        )

    def halo_wait(step, order, slot):
        halo_copy(step, order, slot, slot, sibling, q if step < 2 else 1 - q).wait_recv()

    for order in range(2):
        go(halo_copy(0, order, OWN, 1, (2 * chip(1) + q, z)))
        go(halo_copy(1, order, OWN, 5, (2 * chip(-1) + q, z)))
    for order in range(2):
        go(halo_copy(2, order, OWN, 3 + s, sibling))
    for j in range(1, CHUNKS):
        go(ring_copy(1, 1, j))
        go(ring_copy(-1, 1, CHUNKS - 1 - j))

    def expand_slot(slot, half):
        masks[...] = halo[slot, half, pl.ds(HALF * B, ROWS)].astype(F32)

        @pl.loop(0, HALF)
        def _(j):
            block = halo[slot, half, pl.ds(pl.multiple_of(j * B, B), B)]
            second = masks[pl.ds(j, 1), :].astype(BF16)
            at = slot * ROWS + half * HALF + j
            zexp[at, :, 0:B] = block * (1 - second)
            zexp[at, :, B:WIDE] = block * second

    def expand_both(slot):
        expand_slot(slot, 0)
        expand_slot(slot, 1)

    expand_both(OWN)
    halo_wait(2, 0, 3 - s)
    halo_wait(2, 1, 3 - s)
    expand_both(3 - s)

    def expand_chunk(t, chunk):
        n = group(ORDER[t])
        masks[...] = tags[n].astype(F32)

        @pl.loop(0, CHUNK)
        def _(j):
            block = ring[n, chunk, pl.ds(pl.multiple_of(j * B, B), B)]
            second = masks[pl.ds(chunk * CHUNK + j, 1), :].astype(BF16)
            rows = pl.ds(pl.multiple_of((chunk * CHUNK + j) * B, B), B)
            wide[t, rows, 0:B] = block * (1 - second)
            wide[t, rows, B:WIDE] = block * second

    def forward(distance, j):
        both = ((1, j), (-1, CHUNKS - 1 - j))
        for sense, chunk in both:
            ring_wait(sense, distance, chunk)
            if distance < 3 or (distance == 3 and j < CHUNKS // 2):
                go(ring_copy(sense, distance + 1, chunk))
        if j == 0:
            for sense, chunk in both:
                tag_wait(sense, distance)
                if distance < 3 or sense == 1:
                    go(tag_copy(sense, distance + 1))
        expand_chunk(2 * distance - 1, j)
        expand_chunk(2 * distance, CHUNKS - 1 - j)

    def halo_forward(order):
        halo_wait(0, order, 1)
        halo_wait(1, order, 5)
        go(halo_copy(5, order, 3 - 2 * s, 3 - 3 * s, (2 * chip(s) + 1 - q, z)))
        go(halo_copy(3, order, 1, 1 + s, sibling))
        go(halo_copy(4, order, 5, 5 + s, sibling))

    forward(1, 0)
    halo_forward(0)
    forward(1, 1)
    forward(1, 2)
    halo_forward(1)
    forward(1, 3)
    expand_both(1)
    expand_both(5)
    for order in range(2):
        halo_wait(3, order, 1 - s)
        halo_wait(4, order, 5 - s)
    expand_both(1 - s)
    expand_both(5 - s)

    first_row = (r - OWN) * ROWS

    def place(column):
        return jnp.minimum(lax.rem(column - first_row + NB, NB), SLOTS * ROWS - 1)

    def product_row(i):
        left = jnp.concatenate([fv[i, pl.ds(k * B, B)] for k in range(K)], axis=1)
        right = jnp.concatenate([zexp[place(fcol[i, k])] for k in range(K)], axis=0)
        acc = jnp.dot(left, right, preferred_element_type=F32)
        rows = pl.ds(pl.multiple_of(i * B, B), B)
        for c in range(CB):
            turned[c * B:(c + 1) * B, rows] = jnp.transpose(acc[:, c * B:(c + 1) * B].astype(BF16))

    def product_rows(first):
        for i in range(4):
            product_row(first + i)

    for g in range(4):
        load_f[g].wait()
    near = HALF * (1 - q)
    halo_wait(5, 0, 3 + 3 * s)
    expand_slot(3 + 3 * s, 1 - q)
    product_rows(near)
    forward(2, 0)
    product_rows(near + 4)
    forward(2, 1)
    halo_wait(5, 1, 3 + 3 * s)
    expand_slot(3 + 3 * s, q)
    product_rows(HALF * q)
    forward(2, 2)
    product_rows(HALF * q + 4)
    forward(2, 3)

    def group_of(t):
        return group(ORDER[t])

    pair_copies = []

    def last_product():
        acc = jnp.zeros((WIDE, WIDE), F32)
        for j in range(CHUNKS // 2):
            for sense, chunk in ((1, j), (-1, CHUNKS - 1 - j)):
                ring_wait(sense, 4, chunk)
                expand_chunk(LAST, chunk)
                rows = pl.ds(chunk * CHUNK * B, CHUNK * B)
                acc += jnp.dot(turned[:, rows], wide[LAST, rows], preferred_element_type=F32)
        return acc

    def window(t):
        if t == LAST:
            product = last_product()
        else:
            right = wide[t]
            if t == 0:
                right = zexp[OWN * ROWS:(OWN + 1) * ROWS].reshape(ROWS * B, WIDE)
            product = jnp.dot(turned[...], right, preferred_element_type=F32)
        product = jnp.transpose(product)
        for b in range(4):
            part[t, b % 2, b // 2] = product[b * OUT:(b + 1) * OUT]
        copy = remote(
            part.at[t, 1 - q], other.at[t], pair_send.at[t], pair_recv.at[t], sibling
        )
        pair_copies.append(copy)
        go(copy)

    def sum_copy(t, h):
        d = 2 * group_of(t) + h
        return d, remote(
            chip_sum.at[t, h], arrived.at[m], sum_send.at[t, h], sum_recv.at[m],
            (2 * d + q, z),
        )

    def finish(t):
        pair_copies[t].wait_recv()
        for h in range(2):
            both = part[t, q, h] + other[t, h]
            chip_sum[t, h] = both.astype(BF16)
            d, copy = sum_copy(t, h)

            @pl.when(d == m)
            def _():
                total[...] = both

            @pl.when(d != m)
            def _():
                copy.start()

    window(0)
    early = len(sent)
    forward(3, 0)
    window(1)
    finish(0)
    window(2)
    forward(3, 1)
    finish(1)
    window(3)
    finish(2)
    window(4)
    finish(3)
    finish(4)
    forward(3, 2)
    forward(3, 3)
    window(5)
    window(6)
    finish(5)
    finish(6)
    drain(early)
    tag_wait(1, 4)
    window(7)
    finish(7)

    acc = total[...]
    for j in range(1, CHIPS):
        source = chip(j)
        remote(
            arrived.at[source], arrived.at[source], sum_send.at[0, 0], sum_recv.at[source], sibling
        ).wait_recv()
        acc += arrived[source].astype(F32)
    out[...] = acc

    drain(len(sent))
    for t in range(GROUPS):
        for h in range(2):
            d, copy = sum_copy(t, h)

            @pl.when(d != m)
            def _():
                copy.wait_send()


def body(fblocks, fcol, zblocks, zcol):
    dma = pltpu.SemaphoreType.DMA
    return pl.pallas_call(
        kernel,
        out_shape=pltpu.VMEM((OUT, WIDE), F32),
        in_specs=[pl.BlockSpec(memory_space=pl.ANY)] * 4,
        out_specs=pl.BlockSpec(memory_space=pltpu.VMEM),
        scratch_shapes=[
            pltpu.VMEM((ROWS, K * B, B), BF16),
            pltpu.VMEM((SLOTS, 2, HALF * B + ROWS, B), BF16),
            pltpu.VMEM((SLOTS * ROWS, B, WIDE), BF16),
            pltpu.VMEM((GROUPS, CHUNKS, CHUNK * B, B), BF16),
            pltpu.VMEM((GROUPS, ROWS, B), BF16),
            pltpu.VMEM((GROUPS, ROWS * B, WIDE), BF16),
            pltpu.VMEM((WIDE, ROWS * B), BF16),
            pltpu.VMEM((ROWS, B), F32),
            pltpu.VMEM((GROUPS, 2, 2, OUT, WIDE), F32),
            pltpu.VMEM((GROUPS, 2, OUT, WIDE), F32),
            pltpu.VMEM((GROUPS, 2, OUT, WIDE), BF16),
            pltpu.VMEM((CHIPS, OUT, WIDE), BF16),
            pltpu.VMEM((OUT, WIDE), F32),
            pltpu.SMEM((ROWS, K), jnp.int32),
            pltpu.SMEM((1, ROWS), jnp.int32),
            dma((2,)),
            dma((2,)),
            dma((4,)),
            dma((6, 2)),
            dma((6, 2)),
            dma((2, 4, CHUNKS)),
            dma((2, 4, CHUNKS)),
            dma((2, 4)),
            dma((2, 4)),
            dma((GROUPS,)),
            dma((GROUPS,)),
            dma((GROUPS, 2)),
            dma((CHIPS,)),
        ],
        compiler_params=pltpu.CompilerParams(
            collective_id=0, has_side_effects=True, vmem_limit_bytes=60 * 2**20
        ),
    )(
        fcol,
        zcol.reshape(1, ROWS),
        fblocks.reshape(ROWS, K * B, B),
        zblocks.reshape(ROWS * B, B),
    )


def solution(mesh):
    in_specs = (
        P("rows", None, None, None),
        P("rows", None),
        P("rows", "cols", None, None),
        P("rows", "cols"),
    )
    out_specs = P("rows", "cols")
    return jax.shard_map(body, mesh=mesh, in_specs=in_specs, out_specs=out_specs, check_vma=False)
```

```python
import jax
import jax.numpy as jnp
from jax import lax
from jax.experimental import pallas as pl
from jax.experimental.pallas import tpu as pltpu
from jax.sharding import PartitionSpec as P

B = 128
K = 20
CB = 2
ROWS = 16
CHIPS = 16
GROUPS = 8
NB = 512
SLOTS = 7
OWN = 3
HALF = ROWS // 2
WIDE = CB * B
OUT = 64
CHUNKS = 4
CHUNK = ROWS // CHUNKS
LAST = GROUPS - 1
ORDER = (0, -1, 1, -2, 2, -3, 3, 4)
MESH = pl.DeviceIdType.MESH
F32 = jnp.float32
BF16 = jnp.bfloat16


def kernel(
    fcol_hbm,
    zcol_hbm,
    f_hbm,
    z_hbm,
    out,
    fv,
    halo,
    zexp,
    ring,
    tags,
    wide,
    turned,
    masks,
    part,
    other,
    chip_sum,
    arrived,
    total,
    fcol,
    zcol,
    small_sem,
    z_sem,
    f_sem,
    halo_send,
    halo_recv,
    ring_send,
    ring_recv,
    tag_send,
    tag_recv,
    pair_send,
    pair_recv,
    sum_send,
    sum_recv,
):
    r = lax.axis_index("rows")
    z = lax.axis_index("cols")
    m = lax.div(r, 2)
    q = lax.rem(r, 2)
    s = 2 * q - 1

    def chip(step):
        return lax.rem(m + step + 2 * CHIPS, CHIPS)

    def group(step):
        return lax.rem(z + step + 2 * GROUPS, GROUPS)

    sibling = (r - s, z)

    barrier = pltpu.get_barrier_semaphore()
    peers = [(r, group(1)), (r, group(-1)), sibling, (2 * chip(s) + 1 - q, z)]
    peers += [(2 * chip(j) + q, z) for j in range(1, CHIPS)]
    for peer in peers:
        pl.semaphore_signal(barrier, inc=1, device_id=peer, device_id_type=MESH)

    load_z = []
    for half in range(2):
        load_z.append(
            pltpu.make_async_copy(
                z_hbm.at[pl.ds(half * HALF * B, HALF * B)],
                halo.at[OWN, half, pl.ds(0, HALF * B)],
                z_sem.at[half],
            )
        )
        load_z[-1].start()
    load_zcol = pltpu.make_async_copy(zcol_hbm, zcol, small_sem.at[0])
    load_zcol.start()
    load_fcol = pltpu.make_async_copy(fcol_hbm, fcol, small_sem.at[1])
    load_fcol.start()

    def remote(src, dst, send, recv, device):
        return pltpu.make_async_remote_copy(
            src_ref=src, dst_ref=dst, send_sem=send, recv_sem=recv,
            device_id=device, device_id_type=MESH,
        )

    sent = []

    def go(copy):
        copy.start()
        sent.append(copy)

    def drain(count):
        for copy in sent[:count]:
            copy.wait_send()
        del sent[:count]

    def ring_copy(sense, distance, chunk):
        n = group(-sense * (distance - 1))
        at = (0 if sense == 1 else 1, distance - 1, chunk)
        if distance == 1:
            source = z_hbm.at[pl.ds(chunk * CHUNK * B, CHUNK * B)]
        else:
            source = ring.at[n, chunk]
        return remote(
            source, ring.at[n, chunk], ring_send.at[at], ring_recv.at[at], (r, group(sense))
        )

    def ring_wait(sense, distance, chunk):
        n = group(-sense * distance)
        at = (0 if sense == 1 else 1, distance - 1, chunk)
        remote(
            ring.at[n, chunk], ring.at[n, chunk], ring_send.at[at], ring_recv.at[at],
            (r, group(sense)),
        ).wait_recv()

    def tag_copy(sense, distance):
        n = group(-sense * (distance - 1))
        at = (0 if sense == 1 else 1, distance - 1)
        return remote(
            tags.at[n], tags.at[n], tag_send.at[at], tag_recv.at[at], (r, group(sense))
        )

    def tag_wait(sense, distance):
        n = group(-sense * distance)
        at = (0 if sense == 1 else 1, distance - 1)
        remote(
            tags.at[n], tags.at[n], tag_send.at[at], tag_recv.at[at], (r, group(sense))
        ).wait_recv()

    pl.semaphore_wait(barrier, len(peers))
    go(ring_copy(1, 1, 0))
    go(ring_copy(-1, 1, CHUNKS - 1))

    load_zcol.wait()
    load_fcol.wait()
    row_of = lax.broadcasted_iota(jnp.int32, (ROWS, B), 0)

    def mask_tile(first):
        tile = jnp.zeros((ROWS, B), F32)
        for i in range(first, ROWS):
            tile = jnp.where(row_of == i - first, zcol[0, i].astype(F32), tile)
        return tile.astype(BF16)

    tags[z] = mask_tile(0)
    go(tag_copy(1, 1))
    go(tag_copy(-1, 1))
    halo[OWN, 0, pl.ds(HALF * B, ROWS)] = mask_tile(0)
    halo[OWN, 1, pl.ds(HALF * B, ROWS)] = mask_tile(HALF)
    for half in range(2):
        load_z[half].wait()

    def halo_copy(step, order, src_slot, dst_slot, device, core=q):
        half = core if order == 0 else 1 - core
        return remote(
            halo.at[src_slot, half], halo.at[dst_slot, half],
            halo_send.at[step, order], halo_recv.at[step, order], device,
        )

    def halo_wait(step, order, slot):
        halo_copy(step, order, slot, slot, sibling, q if step < 2 else 1 - q).wait_recv()

    for order in range(2):
        go(halo_copy(0, order, OWN, 1, (2 * chip(1) + q, z)))
        go(halo_copy(1, order, OWN, 5, (2 * chip(-1) + q, z)))
    for order in range(2):
        go(halo_copy(2, order, OWN, 3 + s, sibling))
    for j in range(1, CHUNKS):
        go(ring_copy(1, 1, j))
        go(ring_copy(-1, 1, CHUNKS - 1 - j))

    load_f = []
    for g in range(4):
        rows = pl.ds(4 * g, 4)
        load_f.append(pltpu.make_async_copy(f_hbm.at[rows], fv.at[rows], f_sem.at[g]))
        load_f[-1].start()

    def expand_slot(slot, half):
        masks[...] = halo[slot, half, pl.ds(HALF * B, ROWS)].astype(F32)

        @pl.loop(0, HALF)
        def _(j):
            block = halo[slot, half, pl.ds(pl.multiple_of(j * B, B), B)]
            second = masks[pl.ds(j, 1), :].astype(BF16)
            at = slot * ROWS + half * HALF + j
            zexp[at, :, 0:B] = block * (1 - second)
            zexp[at, :, B:WIDE] = block * second

    def expand_both(slot):
        expand_slot(slot, 0)
        expand_slot(slot, 1)

    expand_both(OWN)
    halo_wait(2, 0, 3 - s)
    halo_wait(2, 1, 3 - s)
    expand_both(3 - s)

    def expand_chunk(t, chunk):
        n = group(ORDER[t])
        masks[...] = tags[n].astype(F32)

        @pl.loop(0, CHUNK)
        def _(j):
            block = ring[n, chunk, pl.ds(pl.multiple_of(j * B, B), B)]
            second = masks[pl.ds(chunk * CHUNK + j, 1), :].astype(BF16)
            rows = pl.ds(pl.multiple_of((chunk * CHUNK + j) * B, B), B)
            wide[t, rows, 0:B] = block * (1 - second)
            wide[t, rows, B:WIDE] = block * second

    def forward(distance, j):
        both = ((1, j), (-1, CHUNKS - 1 - j))
        for sense, chunk in both:
            ring_wait(sense, distance, chunk)
            if distance < 3 or (distance == 3 and j < CHUNKS // 2):
                go(ring_copy(sense, distance + 1, chunk))
        if j == 0:
            for sense, chunk in both:
                tag_wait(sense, distance)
                if distance < 3 or sense == 1:
                    go(tag_copy(sense, distance + 1))
        expand_chunk(2 * distance - 1, j)
        expand_chunk(2 * distance, CHUNKS - 1 - j)

    def halo_forward(order):
        halo_wait(0, order, 1)
        halo_wait(1, order, 5)
        go(halo_copy(5, order, 3 - 2 * s, 3 - 3 * s, (2 * chip(s) + 1 - q, z)))
        go(halo_copy(3, order, 1, 1 + s, sibling))
        go(halo_copy(4, order, 5, 5 + s, sibling))

    forward(1, 0)
    halo_forward(0)
    forward(1, 1)
    forward(1, 2)
    halo_forward(1)
    forward(1, 3)
    expand_both(1)
    expand_both(5)
    for order in range(2):
        halo_wait(3, order, 1 - s)
        halo_wait(4, order, 5 - s)
    expand_both(1 - s)
    expand_both(5 - s)

    first_row = (r - OWN) * ROWS

    def place(column):
        return jnp.minimum(lax.rem(column - first_row + NB, NB), SLOTS * ROWS - 1)

    def product_row(i):
        left = jnp.concatenate([fv[i, pl.ds(k * B, B)] for k in range(K)], axis=1)
        right = jnp.concatenate([zexp[place(fcol[i, k])] for k in range(K)], axis=0)
        acc = jnp.dot(left, right, preferred_element_type=F32)
        rows = pl.ds(pl.multiple_of(i * B, B), B)
        for c in range(CB):
            turned[c * B:(c + 1) * B, rows] = jnp.transpose(acc[:, c * B:(c + 1) * B].astype(BF16))

    def product_rows(first):
        for i in range(4):
            product_row(first + i)

    for g in range(4):
        load_f[g].wait()
    near = HALF * (1 - q)
    halo_wait(5, 0, 3 + 3 * s)
    expand_slot(3 + 3 * s, 1 - q)
    product_rows(near)
    forward(2, 0)
    product_rows(near + 4)
    forward(2, 1)
    halo_wait(5, 1, 3 + 3 * s)
    expand_slot(3 + 3 * s, q)
    product_rows(HALF * q)
    forward(2, 2)
    product_rows(HALF * q + 4)
    forward(2, 3)

    def group_of(t):
        return group(ORDER[t])

    pair_copies = []

    def last_product():
        acc = jnp.zeros((WIDE, WIDE), F32)
        for j in range(CHUNKS // 2):
            for sense, chunk in ((1, j), (-1, CHUNKS - 1 - j)):
                ring_wait(sense, 4, chunk)
                expand_chunk(LAST, chunk)
                rows = pl.ds(chunk * CHUNK * B, CHUNK * B)
                acc += jnp.dot(turned[:, rows], wide[LAST, rows], preferred_element_type=F32)
        return acc

    def window(t):
        if t == LAST:
            product = last_product()
        else:
            right = wide[t]
            if t == 0:
                right = zexp[OWN * ROWS:(OWN + 1) * ROWS].reshape(ROWS * B, WIDE)
            product = jnp.dot(turned[...], right, preferred_element_type=F32)
        product = jnp.transpose(product)
        for b in range(4):
            part[t, b % 2, b // 2] = product[b * OUT:(b + 1) * OUT]
        copy = remote(
            part.at[t, 1 - q], other.at[t], pair_send.at[t], pair_recv.at[t], sibling
        )
        pair_copies.append(copy)
        go(copy)

    def sum_copy(t, h):
        d = 2 * group_of(t) + h
        return d, remote(
            chip_sum.at[t, h], arrived.at[m], sum_send.at[t, h], sum_recv.at[m],
            (2 * d + q, z),
        )

    def finish(t):
        pair_copies[t].wait_recv()
        for h in range(2):
            both = part[t, q, h] + other[t, h]
            chip_sum[t, h] = both.astype(BF16)
            d, copy = sum_copy(t, h)

            @pl.when(d == m)
            def _():
                total[...] = both

            @pl.when(d != m)
            def _():
                copy.start()

    early = len(sent)
    forward(3, 0)
    window(0)
    window(1)
    forward(3, 1)
    finish(0)
    window(2)
    finish(1)
    window(3)
    finish(2)
    window(4)
    finish(3)
    finish(4)
    forward(3, 2)
    forward(3, 3)
    window(5)
    window(6)
    finish(5)
    finish(6)
    drain(early)
    tag_wait(1, 4)
    window(7)
    finish(7)

    acc = total[...]
    for j in range(1, CHIPS):
        source = chip(j)
        remote(
            arrived.at[source], arrived.at[source], sum_send.at[0, 0], sum_recv.at[source], sibling
        ).wait_recv()
        acc += arrived[source].astype(F32)
    out[...] = acc

    drain(len(sent))
    for t in range(GROUPS):
        for h in range(2):
            d, copy = sum_copy(t, h)

            @pl.when(d != m)
            def _():
                copy.wait_send()


def body(fblocks, fcol, zblocks, zcol):
    dma = pltpu.SemaphoreType.DMA
    return pl.pallas_call(
        kernel,
        out_shape=pltpu.VMEM((OUT, WIDE), F32),
        in_specs=[pl.BlockSpec(memory_space=pl.ANY)] * 4,
        out_specs=pl.BlockSpec(memory_space=pltpu.VMEM),
        scratch_shapes=[
            pltpu.VMEM((ROWS, K * B, B), BF16),
            pltpu.VMEM((SLOTS, 2, HALF * B + ROWS, B), BF16),
            pltpu.VMEM((SLOTS * ROWS, B, WIDE), BF16),
            pltpu.VMEM((GROUPS, CHUNKS, CHUNK * B, B), BF16),
            pltpu.VMEM((GROUPS, ROWS, B), BF16),
            pltpu.VMEM((GROUPS, ROWS * B, WIDE), BF16),
            pltpu.VMEM((WIDE, ROWS * B), BF16),
            pltpu.VMEM((ROWS, B), F32),
            pltpu.VMEM((GROUPS, 2, 2, OUT, WIDE), F32),
            pltpu.VMEM((GROUPS, 2, OUT, WIDE), F32),
            pltpu.VMEM((GROUPS, 2, OUT, WIDE), BF16),
            pltpu.VMEM((CHIPS, OUT, WIDE), BF16),
            pltpu.VMEM((OUT, WIDE), F32),
            pltpu.SMEM((ROWS, K), jnp.int32),
            pltpu.SMEM((1, ROWS), jnp.int32),
            dma((2,)),
            dma((2,)),
            dma((4,)),
            dma((6, 2)),
            dma((6, 2)),
            dma((2, 4, CHUNKS)),
            dma((2, 4, CHUNKS)),
            dma((2, 4)),
            dma((2, 4)),
            dma((GROUPS,)),
            dma((GROUPS,)),
            dma((GROUPS, 2)),
            dma((CHIPS,)),
        ],
        compiler_params=pltpu.CompilerParams(
            collective_id=0, has_side_effects=True, vmem_limit_bytes=60 * 2**20
        ),
    )(
        fcol,
        zcol.reshape(1, ROWS),
        fblocks.reshape(ROWS, K * B, B),
        zblocks.reshape(ROWS * B, B),
    )


def solution(mesh):
    in_specs = (
        P("rows", None, None, None),
        P("rows", None),
        P("rows", "cols", None, None),
        P("rows", "cols"),
    )
    out_specs = P("rows", "cols")
    return jax.shard_map(body, mesh=mesh, in_specs=in_specs, out_specs=out_specs, check_vma=False)
```

```python
import jax
import jax.numpy as jnp
from jax import lax
from jax.experimental import pallas as pl
from jax.experimental.pallas import tpu as pltpu
from jax.sharding import PartitionSpec as P

B = 128
K = 20
CB = 2
ROWS = 16
CHIPS = 16
GROUPS = 8
NB = 512
SLOTS = 7
OWN = 3
HALF = ROWS // 2
WIDE = CB * B
OUT = 64
CHUNKS = 4
CHUNK = ROWS // CHUNKS
LAST = GROUPS - 1
ORDER = (0, -1, 1, -2, 2, -3, 3, 4)
MESH = pl.DeviceIdType.MESH
F32 = jnp.float32
BF16 = jnp.bfloat16


def kernel(
    fcol_hbm,
    zcol_hbm,
    f_hbm,
    z_hbm,
    out,
    fv,
    halo,
    zexp,
    ring,
    tags,
    wide,
    turned,
    masks,
    part,
    other,
    chip_sum,
    arrived,
    total,
    fcol,
    zcol,
    small_sem,
    z_sem,
    f_sem,
    halo_send,
    halo_recv,
    ring_send,
    ring_recv,
    tag_send,
    tag_recv,
    pair_send,
    pair_recv,
    sum_send,
    sum_recv,
):
    r = lax.axis_index("rows")
    z = lax.axis_index("cols")
    m = lax.div(r, 2)
    q = lax.rem(r, 2)
    s = 2 * q - 1

    def chip(step):
        return lax.rem(m + step + 2 * CHIPS, CHIPS)

    def group(step):
        return lax.rem(z + step + 2 * GROUPS, GROUPS)

    sibling = (r - s, z)

    barrier = pltpu.get_barrier_semaphore()
    peers = [(r, group(1)), (r, group(-1)), sibling, (2 * chip(s) + 1 - q, z)]
    peers += [(2 * chip(j) + q, z) for j in range(1, CHIPS)]
    for peer in peers:
        pl.semaphore_signal(barrier, inc=1, device_id=peer, device_id_type=MESH)

    load_z = []
    for half in range(2):
        load_z.append(
            pltpu.make_async_copy(
                z_hbm.at[pl.ds(half * HALF * B, HALF * B)],
                halo.at[OWN, half, pl.ds(0, HALF * B)],
                z_sem.at[half],
            )
        )
        load_z[-1].start()
    load_zcol = pltpu.make_async_copy(zcol_hbm, zcol, small_sem.at[0])
    load_zcol.start()
    load_fcol = pltpu.make_async_copy(fcol_hbm, fcol, small_sem.at[1])
    load_fcol.start()

    def remote(src, dst, send, recv, device):
        return pltpu.make_async_remote_copy(
            src_ref=src, dst_ref=dst, send_sem=send, recv_sem=recv,
            device_id=device, device_id_type=MESH,
        )

    sent = []

    def go(copy):
        copy.start()
        sent.append(copy)

    def drain(count):
        for copy in sent[:count]:
            copy.wait_send()
        del sent[:count]

    def ring_copy(sense, distance, chunk):
        n = group(-sense * (distance - 1))
        at = (0 if sense == 1 else 1, distance - 1, chunk)
        if distance == 1:
            source = z_hbm.at[pl.ds(chunk * CHUNK * B, CHUNK * B)]
        else:
            source = ring.at[n, chunk]
        return remote(
            source, ring.at[n, chunk], ring_send.at[at], ring_recv.at[at], (r, group(sense))
        )

    def ring_wait(sense, distance, chunk):
        n = group(-sense * distance)
        at = (0 if sense == 1 else 1, distance - 1, chunk)
        remote(
            ring.at[n, chunk], ring.at[n, chunk], ring_send.at[at], ring_recv.at[at],
            (r, group(sense)),
        ).wait_recv()

    def tag_copy(sense, distance):
        n = group(-sense * (distance - 1))
        at = (0 if sense == 1 else 1, distance - 1)
        return remote(
            tags.at[n], tags.at[n], tag_send.at[at], tag_recv.at[at], (r, group(sense))
        )

    def tag_wait(sense, distance):
        n = group(-sense * distance)
        at = (0 if sense == 1 else 1, distance - 1)
        remote(
            tags.at[n], tags.at[n], tag_send.at[at], tag_recv.at[at], (r, group(sense))
        ).wait_recv()

    pl.semaphore_wait(barrier, len(peers))
    def own_chunk(j):
        return [ring_copy(1, 1, j), ring_copy(-1, 1, CHUNKS - 1 - j)]

    def start(copies):
        for copy in copies:
            copy.start()

    def settle(copies):
        for copy in copies:
            copy.wait_send()

    start(own_chunk(0))

    load_zcol.wait()
    load_fcol.wait()
    row_of = lax.broadcasted_iota(jnp.int32, (ROWS, B), 0)

    def mask_tile(first):
        tile = jnp.zeros((ROWS, B), F32)
        for i in range(first, ROWS):
            tile = jnp.where(row_of == i - first, zcol[0, i].astype(F32), tile)
        return tile.astype(BF16)

    tags[z] = mask_tile(0)
    go(tag_copy(1, 1))
    go(tag_copy(-1, 1))
    halo[OWN, 0, pl.ds(HALF * B, ROWS)] = mask_tile(0)
    halo[OWN, 1, pl.ds(HALF * B, ROWS)] = mask_tile(HALF)
    for half in range(2):
        load_z[half].wait()

    def halo_copy(step, order, src_slot, dst_slot, device, core=q):
        half = core if order == 0 else 1 - core
        return remote(
            halo.at[src_slot, half], halo.at[dst_slot, half],
            halo_send.at[step, order], halo_recv.at[step, order], device,
        )

    def halo_wait(step, order, slot):
        halo_copy(step, order, slot, slot, sibling, q if step < 2 else 1 - q).wait_recv()

    def own_half(order):
        return [
            halo_copy(0, order, OWN, 1, (2 * chip(1) + q, z)),
            halo_copy(1, order, OWN, 5, (2 * chip(-1) + q, z)),
        ]

    start(own_half(0))
    for order in range(2):
        go(halo_copy(2, order, OWN, 3 + s, sibling))
    start(own_chunk(1))

    load_f = []
    for g in range(4):
        rows = pl.ds(4 * g, 4)
        load_f.append(pltpu.make_async_copy(f_hbm.at[rows], fv.at[rows], f_sem.at[g]))
        load_f[-1].start()

    def expand_slot(slot, half):
        masks[...] = halo[slot, half, pl.ds(HALF * B, ROWS)].astype(F32)

        @pl.loop(0, HALF)
        def _(j):
            block = halo[slot, half, pl.ds(pl.multiple_of(j * B, B), B)]
            second = masks[pl.ds(j, 1), :].astype(BF16)
            at = slot * ROWS + half * HALF + j
            zexp[at, :, 0:B] = block * (1 - second)
            zexp[at, :, B:WIDE] = block * second

    def expand_both(slot):
        expand_slot(slot, 0)
        expand_slot(slot, 1)

    expand_both(OWN)
    settle(own_chunk(0))
    start(own_chunk(2))
    halo_wait(2, 0, 3 - s)
    halo_wait(2, 1, 3 - s)
    expand_both(3 - s)
    settle(own_chunk(1))
    start(own_chunk(3))
    settle(own_half(0))
    start(own_half(1))

    def expand_chunk(t, chunk):
        n = group(ORDER[t])
        masks[...] = tags[n].astype(F32)

        @pl.loop(0, CHUNK)
        def _(j):
            block = ring[n, chunk, pl.ds(pl.multiple_of(j * B, B), B)]
            second = masks[pl.ds(chunk * CHUNK + j, 1), :].astype(BF16)
            rows = pl.ds(pl.multiple_of((chunk * CHUNK + j) * B, B), B)
            wide[t, rows, 0:B] = block * (1 - second)
            wide[t, rows, B:WIDE] = block * second

    def forward(distance, j):
        both = ((1, j), (-1, CHUNKS - 1 - j))
        for sense, chunk in both:
            ring_wait(sense, distance, chunk)
            if distance < 3 or (distance == 3 and j < CHUNKS // 2):
                go(ring_copy(sense, distance + 1, chunk))
        if j == 0:
            for sense, chunk in both:
                tag_wait(sense, distance)
                if distance < 3 or sense == 1:
                    go(tag_copy(sense, distance + 1))
        expand_chunk(2 * distance - 1, j)
        expand_chunk(2 * distance, CHUNKS - 1 - j)

    def halo_forward(order):
        halo_wait(0, order, 1)
        halo_wait(1, order, 5)
        go(halo_copy(5, order, 3 - 2 * s, 3 - 3 * s, (2 * chip(s) + 1 - q, z)))
        go(halo_copy(3, order, 1, 1 + s, sibling))
        go(halo_copy(4, order, 5, 5 + s, sibling))

    forward(1, 0)
    halo_forward(0)
    forward(1, 1)
    forward(1, 2)
    halo_forward(1)
    forward(1, 3)
    expand_both(1)
    expand_both(5)
    for order in range(2):
        halo_wait(3, order, 1 - s)
        halo_wait(4, order, 5 - s)
    expand_both(1 - s)
    expand_both(5 - s)

    first_row = (r - OWN) * ROWS

    def place(column):
        return jnp.minimum(lax.rem(column - first_row + NB, NB), SLOTS * ROWS - 1)

    def product_row(i):
        left = jnp.concatenate([fv[i, pl.ds(k * B, B)] for k in range(K)], axis=1)
        right = jnp.concatenate([zexp[place(fcol[i, k])] for k in range(K)], axis=0)
        acc = jnp.dot(left, right, preferred_element_type=F32)
        rows = pl.ds(pl.multiple_of(i * B, B), B)
        for c in range(CB):
            turned[c * B:(c + 1) * B, rows] = jnp.transpose(acc[:, c * B:(c + 1) * B].astype(BF16))

    def product_rows(first):
        for i in range(4):
            product_row(first + i)

    for g in range(4):
        load_f[g].wait()
    near = HALF * (1 - q)
    halo_wait(5, 0, 3 + 3 * s)
    expand_slot(3 + 3 * s, 1 - q)
    product_rows(near)
    forward(2, 0)
    product_rows(near + 4)
    forward(2, 1)
    halo_wait(5, 1, 3 + 3 * s)
    expand_slot(3 + 3 * s, q)
    product_rows(HALF * q)
    forward(2, 2)
    product_rows(HALF * q + 4)
    forward(2, 3)

    def group_of(t):
        return group(ORDER[t])

    pair_copies = []

    def last_product():
        acc = jnp.zeros((WIDE, WIDE), F32)
        for j in range(CHUNKS // 2):
            for sense, chunk in ((1, j), (-1, CHUNKS - 1 - j)):
                ring_wait(sense, 4, chunk)
                expand_chunk(LAST, chunk)
                rows = pl.ds(chunk * CHUNK * B, CHUNK * B)
                acc += jnp.dot(turned[:, rows], wide[LAST, rows], preferred_element_type=F32)
        return acc

    def window(t):
        if t == LAST:
            product = last_product()
        else:
            right = wide[t]
            if t == 0:
                right = zexp[OWN * ROWS:(OWN + 1) * ROWS].reshape(ROWS * B, WIDE)
            product = jnp.dot(turned[...], right, preferred_element_type=F32)
        product = jnp.transpose(product)
        for b in range(4):
            part[t, b % 2, b // 2] = product[b * OUT:(b + 1) * OUT]
        copy = remote(
            part.at[t, 1 - q], other.at[t], pair_send.at[t], pair_recv.at[t], sibling
        )
        pair_copies.append(copy)
        go(copy)

    def sum_copy(t, h):
        d = 2 * group_of(t) + h
        return d, remote(
            chip_sum.at[t, h], arrived.at[m], sum_send.at[t, h], sum_recv.at[m],
            (2 * d + q, z),
        )

    def finish(t):
        pair_copies[t].wait_recv()
        for h in range(2):
            both = part[t, q, h] + other[t, h]
            chip_sum[t, h] = both.astype(BF16)
            d, copy = sum_copy(t, h)

            @pl.when(d == m)
            def _():
                total[...] = both

            @pl.when(d != m)
            def _():
                copy.start()

    early = len(sent)
    forward(3, 0)
    window(0)
    window(1)
    forward(3, 1)
    finish(0)
    window(2)
    finish(1)
    window(3)
    finish(2)
    window(4)
    finish(3)
    finish(4)
    forward(3, 2)
    forward(3, 3)
    window(5)
    window(6)
    finish(5)
    finish(6)
    drain(early)
    settle(own_chunk(2) + own_chunk(3) + own_half(1))
    tag_wait(1, 4)
    window(7)
    finish(7)

    acc = total[...]
    for j in range(1, CHIPS):
        source = chip(j)
        remote(
            arrived.at[source], arrived.at[source], sum_send.at[0, 0], sum_recv.at[source], sibling
        ).wait_recv()
        acc += arrived[source].astype(F32)
    out[...] = acc

    drain(len(sent))
    for t in range(GROUPS):
        for h in range(2):
            d, copy = sum_copy(t, h)

            @pl.when(d != m)
            def _():
                copy.wait_send()


def body(fblocks, fcol, zblocks, zcol):
    dma = pltpu.SemaphoreType.DMA
    return pl.pallas_call(
        kernel,
        out_shape=pltpu.VMEM((OUT, WIDE), F32),
        in_specs=[pl.BlockSpec(memory_space=pl.ANY)] * 4,
        out_specs=pl.BlockSpec(memory_space=pltpu.VMEM),
        scratch_shapes=[
            pltpu.VMEM((ROWS, K * B, B), BF16),
            pltpu.VMEM((SLOTS, 2, HALF * B + ROWS, B), BF16),
            pltpu.VMEM((SLOTS * ROWS, B, WIDE), BF16),
            pltpu.VMEM((GROUPS, CHUNKS, CHUNK * B, B), BF16),
            pltpu.VMEM((GROUPS, ROWS, B), BF16),
            pltpu.VMEM((GROUPS, ROWS * B, WIDE), BF16),
            pltpu.VMEM((WIDE, ROWS * B), BF16),
            pltpu.VMEM((ROWS, B), F32),
            pltpu.VMEM((GROUPS, 2, 2, OUT, WIDE), F32),
            pltpu.VMEM((GROUPS, 2, OUT, WIDE), F32),
            pltpu.VMEM((GROUPS, 2, OUT, WIDE), BF16),
            pltpu.VMEM((CHIPS, OUT, WIDE), BF16),
            pltpu.VMEM((OUT, WIDE), F32),
            pltpu.SMEM((ROWS, K), jnp.int32),
            pltpu.SMEM((1, ROWS), jnp.int32),
            dma((2,)),
            dma((2,)),
            dma((4,)),
            dma((6, 2)),
            dma((6, 2)),
            dma((2, 4, CHUNKS)),
            dma((2, 4, CHUNKS)),
            dma((2, 4)),
            dma((2, 4)),
            dma((GROUPS,)),
            dma((GROUPS,)),
            dma((GROUPS, 2)),
            dma((CHIPS,)),
        ],
        compiler_params=pltpu.CompilerParams(
            collective_id=0, has_side_effects=True, vmem_limit_bytes=60 * 2**20
        ),
    )(
        fcol,
        zcol.reshape(1, ROWS),
        fblocks.reshape(ROWS, K * B, B),
        zblocks.reshape(ROWS * B, B),
    )


def solution(mesh):
    in_specs = (
        P("rows", None, None, None),
        P("rows", None),
        P("rows", "cols", None, None),
        P("rows", "cols"),
    )
    out_specs = P("rows", "cols")
    return jax.shard_map(body, mesh=mesh, in_specs=in_specs, out_specs=out_specs, check_vma=False)
```

```python
import jax
import jax.numpy as jnp
from jax import lax
from jax.experimental import pallas as pl
from jax.experimental.pallas import tpu as pltpu
from jax.sharding import PartitionSpec as P

B = 128
K = 20
CB = 2
ROWS = 16
CHIPS = 16
GROUPS = 8
NB = 512
SLOTS = 7
OWN = 3
HALF = ROWS // 2
WIDE = CB * B
OUT = 64
CHUNKS = 4
CHUNK = ROWS // CHUNKS
LAST = GROUPS - 1
ORDER = (0, -1, 1, -2, 2, -3, 3, 4)
MESH = pl.DeviceIdType.MESH
F32 = jnp.float32
BF16 = jnp.bfloat16


def kernel(
    fcol_hbm,
    zcol_hbm,
    f_hbm,
    z_hbm,
    out,
    fv,
    halo,
    zexp,
    ring,
    tags,
    wide,
    turned,
    masks,
    part,
    other,
    chip_sum,
    arrived,
    total,
    fcol,
    zcol,
    small_sem,
    z_sem,
    f_sem,
    halo_send,
    halo_recv,
    ring_send,
    ring_recv,
    tag_send,
    tag_recv,
    pair_send,
    pair_recv,
    sum_send,
    sum_recv,
):
    r = lax.axis_index("rows")
    z = lax.axis_index("cols")
    m = lax.div(r, 2)
    q = lax.rem(r, 2)
    s = 2 * q - 1

    def chip(step):
        return lax.rem(m + step + 2 * CHIPS, CHIPS)

    def group(step):
        return lax.rem(z + step + 2 * GROUPS, GROUPS)

    sibling = (r - s, z)

    load_z = []
    for half in range(2):
        load_z.append(
            pltpu.make_async_copy(
                z_hbm.at[pl.ds(half * HALF * B, HALF * B)],
                halo.at[OWN, half, pl.ds(0, HALF * B)],
                z_sem.at[half],
            )
        )
        load_z[-1].start()
    load_zcol = pltpu.make_async_copy(zcol_hbm, zcol, small_sem.at[0])
    load_zcol.start()
    load_fcol = pltpu.make_async_copy(fcol_hbm, fcol, small_sem.at[1])
    load_fcol.start()
    load_f = []
    for g in range(4):
        rows = pl.ds(4 * g, 4)
        load_f.append(pltpu.make_async_copy(f_hbm.at[rows], fv.at[rows], f_sem.at[g]))
        load_f[-1].start()

    barrier = pltpu.get_barrier_semaphore()
    peers = [(r, group(1)), (r, group(-1)), sibling, (2 * chip(s) + 1 - q, z)]
    peers += [(2 * chip(j) + q, z) for j in range(1, CHIPS)]
    for peer in peers:
        pl.semaphore_signal(barrier, inc=1, device_id=peer, device_id_type=MESH)

    def remote(src, dst, send, recv, device):
        return pltpu.make_async_remote_copy(
            src_ref=src, dst_ref=dst, send_sem=send, recv_sem=recv,
            device_id=device, device_id_type=MESH,
        )

    sent = []

    def go(copy):
        copy.start()
        sent.append(copy)

    def drain(count):
        for copy in sent[:count]:
            copy.wait_send()
        del sent[:count]

    def ring_copy(sense, distance, chunk):
        n = group(-sense * (distance - 1))
        at = (0 if sense == 1 else 1, distance - 1, chunk)
        if distance == 1:
            source = z_hbm.at[pl.ds(chunk * CHUNK * B, CHUNK * B)]
        else:
            source = ring.at[n, chunk]
        return remote(
            source, ring.at[n, chunk], ring_send.at[at], ring_recv.at[at], (r, group(sense))
        )

    def ring_wait(sense, distance, chunk):
        n = group(-sense * distance)
        at = (0 if sense == 1 else 1, distance - 1, chunk)
        remote(
            ring.at[n, chunk], ring.at[n, chunk], ring_send.at[at], ring_recv.at[at],
            (r, group(sense)),
        ).wait_recv()

    def tag_copy(sense, distance):
        n = group(-sense * (distance - 1))
        at = (0 if sense == 1 else 1, distance - 1)
        return remote(
            tags.at[n], tags.at[n], tag_send.at[at], tag_recv.at[at], (r, group(sense))
        )

    def tag_wait(sense, distance):
        n = group(-sense * distance)
        at = (0 if sense == 1 else 1, distance - 1)
        remote(
            tags.at[n], tags.at[n], tag_send.at[at], tag_recv.at[at], (r, group(sense))
        ).wait_recv()

    pl.semaphore_wait(barrier, len(peers))
    go(ring_copy(1, 1, 0))
    go(ring_copy(-1, 1, CHUNKS - 1))

    load_zcol.wait()
    load_fcol.wait()
    row_of = lax.broadcasted_iota(jnp.int32, (ROWS, B), 0)

    def mask_tile(first):
        tile = jnp.zeros((ROWS, B), F32)
        for i in range(first, ROWS):
            tile = jnp.where(row_of == i - first, zcol[0, i].astype(F32), tile)
        return tile.astype(BF16)

    tags[z] = mask_tile(0)
    go(tag_copy(1, 1))
    go(tag_copy(-1, 1))
    halo[OWN, 0, pl.ds(HALF * B, ROWS)] = mask_tile(0)
    halo[OWN, 1, pl.ds(HALF * B, ROWS)] = mask_tile(HALF)
    for half in range(2):
        load_z[half].wait()

    def halo_copy(step, order, src_slot, dst_slot, device, core=q):
        half = core if order == 0 else 1 - core
        return remote(
            halo.at[src_slot, half], halo.at[dst_slot, half],
            halo_send.at[step, order], halo_recv.at[step, order], device,
        )

    def halo_wait(step, order, slot):
        halo_copy(step, order, slot, slot, sibling, q if step < 2 else 1 - q).wait_recv()

    for order in range(2):
        go(halo_copy(0, order, OWN, 1, (2 * chip(1) + q, z)))
        go(halo_copy(1, order, OWN, 5, (2 * chip(-1) + q, z)))
    for order in range(2):
        go(halo_copy(2, order, OWN, 3 + s, sibling))
    for j in range(1, CHUNKS):
        go(ring_copy(1, 1, j))
        go(ring_copy(-1, 1, CHUNKS - 1 - j))

    def expand_slot(slot, half):
        masks[...] = halo[slot, half, pl.ds(HALF * B, ROWS)].astype(F32)

        @pl.loop(0, HALF)
        def _(j):
            block = halo[slot, half, pl.ds(pl.multiple_of(j * B, B), B)]
            second = masks[pl.ds(j, 1), :].astype(BF16)
            at = slot * ROWS + half * HALF + j
            zexp[at, :, 0:B] = block * (1 - second)
            zexp[at, :, B:WIDE] = block * second

    def expand_both(slot):
        expand_slot(slot, 0)
        expand_slot(slot, 1)

    expand_both(OWN)
    halo_wait(2, 0, 3 - s)
    halo_wait(2, 1, 3 - s)
    expand_both(3 - s)

    def expand_chunk(t, chunk):
        n = group(ORDER[t])
        masks[...] = tags[n].astype(F32)

        @pl.loop(0, CHUNK)
        def _(j):
            block = ring[n, chunk, pl.ds(pl.multiple_of(j * B, B), B)]
            second = masks[pl.ds(chunk * CHUNK + j, 1), :].astype(BF16)
            rows = pl.ds(pl.multiple_of((chunk * CHUNK + j) * B, B), B)
            wide[t, rows, 0:B] = block * (1 - second)
            wide[t, rows, B:WIDE] = block * second

    def forward(distance, j):
        both = ((1, j), (-1, CHUNKS - 1 - j))
        for sense, chunk in both:
            ring_wait(sense, distance, chunk)
            if distance < 3 or (distance == 3 and j < CHUNKS // 2):
                go(ring_copy(sense, distance + 1, chunk))
        if j == 0:
            for sense, chunk in both:
                tag_wait(sense, distance)
                if distance < 3 or sense == 1:
                    go(tag_copy(sense, distance + 1))
        expand_chunk(2 * distance - 1, j)
        expand_chunk(2 * distance, CHUNKS - 1 - j)

    def halo_forward(order):
        halo_wait(0, order, 1)
        halo_wait(1, order, 5)
        go(halo_copy(5, order, 3 - 2 * s, 3 - 3 * s, (2 * chip(s) + 1 - q, z)))
        go(halo_copy(3, order, 1, 1 + s, sibling))
        go(halo_copy(4, order, 5, 5 + s, sibling))

    forward(1, 0)
    halo_forward(0)
    forward(1, 1)
    forward(1, 2)
    halo_forward(1)
    forward(1, 3)
    expand_both(1)
    expand_both(5)
    for order in range(2):
        halo_wait(3, order, 1 - s)
        halo_wait(4, order, 5 - s)
    expand_both(1 - s)
    expand_both(5 - s)

    first_row = (r - OWN) * ROWS

    def place(column):
        return jnp.minimum(lax.rem(column - first_row + NB, NB), SLOTS * ROWS - 1)

    def product_row(i):
        left = jnp.concatenate([fv[i, pl.ds(k * B, B)] for k in range(K)], axis=1)
        right = jnp.concatenate([zexp[place(fcol[i, k])] for k in range(K)], axis=0)
        acc = jnp.dot(left, right, preferred_element_type=F32)
        rows = pl.ds(pl.multiple_of(i * B, B), B)
        for c in range(CB):
            turned[c * B:(c + 1) * B, rows] = jnp.transpose(acc[:, c * B:(c + 1) * B].astype(BF16))

    def product_rows(first):
        for i in range(4):
            product_row(first + i)

    for g in range(4):
        load_f[g].wait()
    near = HALF * (1 - q)
    halo_wait(5, 0, 3 + 3 * s)
    expand_slot(3 + 3 * s, 1 - q)
    product_rows(near)
    forward(2, 0)
    product_rows(near + 4)
    forward(2, 1)
    halo_wait(5, 1, 3 + 3 * s)
    expand_slot(3 + 3 * s, q)
    product_rows(HALF * q)
    forward(2, 2)
    product_rows(HALF * q + 4)
    forward(2, 3)

    def group_of(t):
        return group(ORDER[t])

    pair_copies = []

    def last_product():
        acc = jnp.zeros((WIDE, WIDE), F32)
        for j in range(CHUNKS // 2):
            for sense, chunk in ((1, j), (-1, CHUNKS - 1 - j)):
                ring_wait(sense, 4, chunk)
                expand_chunk(LAST, chunk)
                acc += part_product(LAST, chunk, 1)
        return acc

    def part_product(t, first, count):
        rows = pl.ds(first * CHUNK * B, count * CHUNK * B)
        return jnp.dot(turned[:, rows], wide[t, rows], preferred_element_type=F32)

    def window(t, product=None):
        if t == LAST:
            product = last_product()
        elif product is None:
            right = wide[t]
            if t == 0:
                right = zexp[OWN * ROWS:(OWN + 1) * ROWS].reshape(ROWS * B, WIDE)
            product = jnp.dot(turned[...], right, preferred_element_type=F32)
        product = jnp.transpose(product)
        for b in range(4):
            part[t, b % 2, b // 2] = product[b * OUT:(b + 1) * OUT]
        copy = remote(
            part.at[t, 1 - q], other.at[t], pair_send.at[t], pair_recv.at[t], sibling
        )
        pair_copies.append(copy)
        go(copy)

    def sum_copy(t, h):
        d = 2 * group_of(t) + h
        return d, remote(
            chip_sum.at[t, h], arrived.at[m], sum_send.at[t, h], sum_recv.at[m],
            (2 * d + q, z),
        )

    def finish(t):
        pair_copies[t].wait_recv()
        for h in range(2):
            both = part[t, q, h] + other[t, h]
            chip_sum[t, h] = both.astype(BF16)
            d, copy = sum_copy(t, h)

            @pl.when(d == m)
            def _():
                total[...] = both

            @pl.when(d != m)
            def _():
                copy.start()

    window(0)
    early = len(sent)
    forward(3, 0)
    window(1)
    finish(0)
    window(2)
    forward(3, 1)
    finish(1)
    window(3)
    finish(2)
    window(4)
    finish(3)
    finish(4)
    forward(3, 2)
    head5 = part_product(5, 0, CHUNKS - 1)
    head6 = part_product(6, 1, CHUNKS - 1)
    forward(3, 3)
    window(5, head5 + part_product(5, CHUNKS - 1, 1))
    window(6, head6 + part_product(6, 0, 1))
    finish(5)
    finish(6)
    drain(early)
    tag_wait(1, 4)
    window(7)
    finish(7)

    acc = total[...]
    for j in range(1, CHIPS):
        source = chip(j)
        remote(
            arrived.at[source], arrived.at[source], sum_send.at[0, 0], sum_recv.at[source], sibling
        ).wait_recv()
        acc += arrived[source].astype(F32)
    out[...] = acc

    drain(len(sent))
    for t in range(GROUPS):
        for h in range(2):
            d, copy = sum_copy(t, h)

            @pl.when(d != m)
            def _():
                copy.wait_send()


def body(fblocks, fcol, zblocks, zcol):
    dma = pltpu.SemaphoreType.DMA
    return pl.pallas_call(
        kernel,
        out_shape=pltpu.VMEM((OUT, WIDE), F32),
        in_specs=[pl.BlockSpec(memory_space=pl.ANY)] * 4,
        out_specs=pl.BlockSpec(memory_space=pltpu.VMEM),
        scratch_shapes=[
            pltpu.VMEM((ROWS, K * B, B), BF16),
            pltpu.VMEM((SLOTS, 2, HALF * B + ROWS, B), BF16),
            pltpu.VMEM((SLOTS * ROWS, B, WIDE), BF16),
            pltpu.VMEM((GROUPS, CHUNKS, CHUNK * B, B), BF16),
            pltpu.VMEM((GROUPS, ROWS, B), BF16),
            pltpu.VMEM((GROUPS, ROWS * B, WIDE), BF16),
            pltpu.VMEM((WIDE, ROWS * B), BF16),
            pltpu.VMEM((ROWS, B), F32),
            pltpu.VMEM((GROUPS, 2, 2, OUT, WIDE), F32),
            pltpu.VMEM((GROUPS, 2, OUT, WIDE), F32),
            pltpu.VMEM((GROUPS, 2, OUT, WIDE), BF16),
            pltpu.VMEM((CHIPS, OUT, WIDE), BF16),
            pltpu.VMEM((OUT, WIDE), F32),
            pltpu.SMEM((ROWS, K), jnp.int32),
            pltpu.SMEM((1, ROWS), jnp.int32),
            dma((2,)),
            dma((2,)),
            dma((4,)),
            dma((6, 2)),
            dma((6, 2)),
            dma((2, 4, CHUNKS)),
            dma((2, 4, CHUNKS)),
            dma((2, 4)),
            dma((2, 4)),
            dma((GROUPS,)),
            dma((GROUPS,)),
            dma((GROUPS, 2)),
            dma((CHIPS,)),
        ],
        compiler_params=pltpu.CompilerParams(
            collective_id=0, has_side_effects=True, vmem_limit_bytes=60 * 2**20
        ),
    )(
        fcol,
        zcol.reshape(1, ROWS),
        fblocks.reshape(ROWS, K * B, B),
        zblocks.reshape(ROWS * B, B),
    )


def solution(mesh):
    in_specs = (
        P("rows", None, None, None),
        P("rows", None),
        P("rows", "cols", None, None),
        P("rows", "cols"),
    )
    out_specs = P("rows", "cols")
    return jax.shard_map(body, mesh=mesh, in_specs=in_specs, out_specs=out_specs, check_vma=False)
```

```python
import jax
import jax.numpy as jnp
from jax import lax
from jax.experimental import pallas as pl
from jax.experimental.pallas import tpu as pltpu
from jax.sharding import PartitionSpec as P

B = 128
K = 20
CB = 2
ROWS = 16
CHIPS = 16
GROUPS = 8
NB = 512
SLOTS = 7
OWN = 3
HALF = ROWS // 2
WIDE = CB * B
OUT = 64
CHUNKS = 4
CHUNK = ROWS // CHUNKS
LAST = GROUPS - 1
ORDER = (0, -1, 1, -2, 2, -3, 3, 4)
MESH = pl.DeviceIdType.MESH
F32 = jnp.float32
BF16 = jnp.bfloat16


def kernel(
    fcol_hbm,
    zcol_hbm,
    f_hbm,
    z_hbm,
    out,
    fv,
    halo,
    zexp,
    ring,
    tags,
    wide,
    turned,
    masks,
    part,
    other,
    chip_sum,
    arrived,
    total,
    fcol,
    zcol,
    small_sem,
    z_sem,
    f_sem,
    halo_send,
    halo_recv,
    ring_send,
    ring_recv,
    tag_send,
    tag_recv,
    pair_send,
    pair_recv,
    sum_send,
    sum_recv,
):
    r = lax.axis_index("rows")
    z = lax.axis_index("cols")
    m = lax.div(r, 2)
    q = lax.rem(r, 2)
    s = 2 * q - 1

    def chip(step):
        return lax.rem(m + step + 2 * CHIPS, CHIPS)

    def group(step):
        return lax.rem(z + step + 2 * GROUPS, GROUPS)

    sibling = (r - s, z)

    load_z = []
    for half in range(2):
        load_z.append(
            pltpu.make_async_copy(
                z_hbm.at[pl.ds(half * HALF * B, HALF * B)],
                halo.at[OWN, half, pl.ds(0, HALF * B)],
                z_sem.at[half],
            )
        )
        load_z[-1].start()
    load_zcol = pltpu.make_async_copy(zcol_hbm, zcol, small_sem.at[0])
    load_zcol.start()
    load_fcol = pltpu.make_async_copy(fcol_hbm, fcol, small_sem.at[1])
    load_fcol.start()
    load_f = []
    for g in range(4):
        rows = pl.ds(4 * g, 4)
        load_f.append(pltpu.make_async_copy(f_hbm.at[rows], fv.at[rows], f_sem.at[g]))
        load_f[-1].start()

    barrier = pltpu.get_barrier_semaphore()
    peers = [(r, group(1)), (r, group(-1)), sibling, (2 * chip(s) + 1 - q, z)]
    peers += [(2 * chip(j) + q, z) for j in range(1, CHIPS)]
    for peer in peers:
        pl.semaphore_signal(barrier, inc=1, device_id=peer, device_id_type=MESH)

    def remote(src, dst, send, recv, device):
        return pltpu.make_async_remote_copy(
            src_ref=src, dst_ref=dst, send_sem=send, recv_sem=recv,
            device_id=device, device_id_type=MESH,
        )

    sent = []

    def go(copy):
        copy.start()
        sent.append(copy)

    def drain(count):
        for copy in sent[:count]:
            copy.wait_send()
        del sent[:count]

    def ring_copy(sense, distance, chunk):
        n = group(-sense * (distance - 1))
        at = (0 if sense == 1 else 1, distance - 1, chunk)
        if distance == 1:
            source = z_hbm.at[pl.ds(chunk * CHUNK * B, CHUNK * B)]
        else:
            source = ring.at[n, chunk]
        return remote(
            source, ring.at[n, chunk], ring_send.at[at], ring_recv.at[at], (r, group(sense))
        )

    def ring_wait(sense, distance, chunk):
        n = group(-sense * distance)
        at = (0 if sense == 1 else 1, distance - 1, chunk)
        remote(
            ring.at[n, chunk], ring.at[n, chunk], ring_send.at[at], ring_recv.at[at],
            (r, group(sense)),
        ).wait_recv()

    def tag_copy(sense, distance):
        n = group(-sense * (distance - 1))
        at = (0 if sense == 1 else 1, distance - 1)
        return remote(
            tags.at[n], tags.at[n], tag_send.at[at], tag_recv.at[at], (r, group(sense))
        )

    def tag_wait(sense, distance):
        n = group(-sense * distance)
        at = (0 if sense == 1 else 1, distance - 1)
        remote(
            tags.at[n], tags.at[n], tag_send.at[at], tag_recv.at[at], (r, group(sense))
        ).wait_recv()

    pl.semaphore_wait(barrier, len(peers))
    go(ring_copy(1, 1, 0))
    go(ring_copy(-1, 1, CHUNKS - 1))

    load_zcol.wait()
    load_fcol.wait()
    row_of = lax.broadcasted_iota(jnp.int32, (ROWS, B), 0)

    def mask_tile(first):
        tile = jnp.zeros((ROWS, B), F32)
        for i in range(first, ROWS):
            tile = jnp.where(row_of == i - first, zcol[0, i].astype(F32), tile)
        return tile.astype(BF16)

    tags[z] = mask_tile(0)
    go(tag_copy(1, 1))
    go(tag_copy(-1, 1))
    halo[OWN, 0, pl.ds(HALF * B, ROWS)] = mask_tile(0)
    halo[OWN, 1, pl.ds(HALF * B, ROWS)] = mask_tile(HALF)
    for half in range(2):
        load_z[half].wait()

    def halo_copy(step, order, src_slot, dst_slot, device, core=q):
        half = core if order == 0 else 1 - core
        return remote(
            halo.at[src_slot, half], halo.at[dst_slot, half],
            halo_send.at[step, order], halo_recv.at[step, order], device,
        )

    def halo_wait(step, order, slot):
        halo_copy(step, order, slot, slot, sibling, q if step < 2 else 1 - q).wait_recv()

    for order in range(2):
        go(halo_copy(0, order, OWN, 1, (2 * chip(1) + q, z)))
        go(halo_copy(1, order, OWN, 5, (2 * chip(-1) + q, z)))
    for order in range(2):
        go(halo_copy(2, order, OWN, 3 + s, sibling))
    for j in range(1, CHUNKS):
        go(ring_copy(1, 1, j))
        go(ring_copy(-1, 1, CHUNKS - 1 - j))

    def expand_slot(slot, half):
        masks[...] = halo[slot, half, pl.ds(HALF * B, ROWS)].astype(F32)

        @pl.loop(0, HALF)
        def _(j):
            block = halo[slot, half, pl.ds(pl.multiple_of(j * B, B), B)]
            second = masks[pl.ds(j, 1), :].astype(BF16)
            at = slot * ROWS + half * HALF + j
            zexp[at, :, 0:B] = block * (1 - second)
            zexp[at, :, B:WIDE] = block * second

    def expand_both(slot):
        expand_slot(slot, 0)
        expand_slot(slot, 1)

    expand_both(OWN)
    halo_wait(2, 0, 3 - s)
    halo_wait(2, 1, 3 - s)
    expand_both(3 - s)

    def expand_chunk(t, chunk):
        n = group(ORDER[t])
        masks[...] = tags[n].astype(F32)

        @pl.loop(0, CHUNK)
        def _(j):
            block = ring[n, chunk, pl.ds(pl.multiple_of(j * B, B), B)]
            second = masks[pl.ds(chunk * CHUNK + j, 1), :].astype(BF16)
            rows = pl.ds(pl.multiple_of((chunk * CHUNK + j) * B, B), B)
            wide[t, rows, 0:B] = block * (1 - second)
            wide[t, rows, B:WIDE] = block * second

    def forward(distance, j):
        both = ((1, j), (-1, CHUNKS - 1 - j))
        for sense, chunk in both:
            ring_wait(sense, distance, chunk)
            if distance < 3 or (distance == 3 and j < CHUNKS // 2):
                go(ring_copy(sense, distance + 1, chunk))
        if j == 0:
            for sense, chunk in both:
                tag_wait(sense, distance)
                if distance < 3 or sense == 1:
                    go(tag_copy(sense, distance + 1))
        expand_chunk(2 * distance - 1, j)
        expand_chunk(2 * distance, CHUNKS - 1 - j)

    def halo_forward(order):
        halo_wait(0, order, 1)
        halo_wait(1, order, 5)
        go(halo_copy(5, order, 3 - 2 * s, 3 - 3 * s, (2 * chip(s) + 1 - q, z)))
        go(halo_copy(3, order, 1, 1 + s, sibling))
        go(halo_copy(4, order, 5, 5 + s, sibling))

    forward(1, 0)
    halo_forward(0)
    forward(1, 1)
    forward(1, 2)
    halo_forward(1)
    forward(1, 3)
    expand_both(1)
    expand_both(5)
    for order in range(2):
        halo_wait(3, order, 1 - s)
        halo_wait(4, order, 5 - s)
    expand_both(1 - s)
    expand_both(5 - s)

    first_row = (r - OWN) * ROWS

    def place(column):
        return jnp.minimum(lax.rem(column - first_row + NB, NB), SLOTS * ROWS - 1)

    def product_row(i):
        left = jnp.concatenate([fv[i, pl.ds(k * B, B)] for k in range(K)], axis=1)
        right = jnp.concatenate([zexp[place(fcol[i, k])] for k in range(K)], axis=0)
        acc = jnp.dot(left, right, preferred_element_type=F32)
        rows = pl.ds(pl.multiple_of(i * B, B), B)
        for c in range(CB):
            turned[c * B:(c + 1) * B, rows] = jnp.transpose(acc[:, c * B:(c + 1) * B].astype(BF16))

    def product_rows(first):
        for i in range(4):
            product_row(first + i)

    for g in range(4):
        load_f[g].wait()
    near = HALF * (1 - q)
    halo_wait(5, 0, 3 + 3 * s)
    expand_slot(3 + 3 * s, 1 - q)
    product_rows(near)
    forward(2, 0)
    product_rows(near + 4)
    forward(2, 1)
    halo_wait(5, 1, 3 + 3 * s)
    expand_slot(3 + 3 * s, q)
    product_rows(HALF * q)
    forward(2, 2)
    product_rows(HALF * q + 4)
    forward(2, 3)

    def group_of(t):
        return group(ORDER[t])

    pair_copies = []

    def last_product():
        acc = jnp.zeros((WIDE, WIDE), F32)
        for j in range(CHUNKS // 2):
            for sense, chunk in ((1, j), (-1, CHUNKS - 1 - j)):
                ring_wait(sense, 4, chunk)
                expand_chunk(LAST, chunk)
                rows = pl.ds(chunk * CHUNK * B, CHUNK * B)
                acc += jnp.dot(turned[:, rows], wide[LAST, rows], preferred_element_type=F32)
        return acc

    def window(t):
        if t == LAST:
            product = last_product()
        else:
            right = wide[t]
            if t == 0:
                right = zexp[OWN * ROWS:(OWN + 1) * ROWS].reshape(ROWS * B, WIDE)
            product = jnp.dot(turned[...], right, preferred_element_type=F32)
        product = jnp.transpose(product)
        for b in range(4):
            part[t, b % 2, b // 2] = product[b * OUT:(b + 1) * OUT]
        copy = remote(
            part.at[t, 1 - q], other.at[t], pair_send.at[t], pair_recv.at[t], sibling
        )
        pair_copies.append(copy)
        go(copy)

    def sum_copy(t, h):
        d = 2 * group_of(t) + h
        return d, remote(
            chip_sum.at[t, h], arrived.at[m], sum_send.at[t, h], sum_recv.at[m],
            (2 * d + q, z),
        )

    def finish(t):
        pair_copies[t].wait_recv()
        for h in range(2):
            both = part[t, q, h] + other[t, h]
            chip_sum[t, h] = both.astype(BF16)
            d, copy = sum_copy(t, h)

            @pl.when(d == m)
            def _():
                total[...] = both

            @pl.when(d != m)
            def _():
                copy.start()

    window(0)
    early = len(sent)
    forward(3, 0)
    window(1)
    finish(0)
    window(2)
    forward(3, 1)
    finish(1)
    window(3)
    finish(2)
    window(4)
    finish(3)
    finish(4)
    forward(3, 2)
    forward(3, 3)
    window(5)
    window(6)
    finish(5)
    finish(6)
    drain(early)
    tag_wait(1, 4)
    window(7)
    drain(len(sent) - 1)
    finish(7)

    drain(len(sent))
    for t in range(GROUPS):
        for h in range(2):
            d, copy = sum_copy(t, h)

            @pl.when(d != m)
            def _():
                copy.wait_send()

    acc = total[...]
    for j in range(1, CHIPS):
        source = chip(j)
        remote(
            arrived.at[source], arrived.at[source], sum_send.at[0, 0], sum_recv.at[source], sibling
        ).wait_recv()
        acc += arrived[source].astype(F32)
    out[...] = acc


def body(fblocks, fcol, zblocks, zcol):
    dma = pltpu.SemaphoreType.DMA
    return pl.pallas_call(
        kernel,
        out_shape=pltpu.VMEM((OUT, WIDE), F32),
        in_specs=[pl.BlockSpec(memory_space=pl.ANY)] * 4,
        out_specs=pl.BlockSpec(memory_space=pltpu.VMEM),
        scratch_shapes=[
            pltpu.VMEM((ROWS, K * B, B), BF16),
            pltpu.VMEM((SLOTS, 2, HALF * B + ROWS, B), BF16),
            pltpu.VMEM((SLOTS * ROWS, B, WIDE), BF16),
            pltpu.VMEM((GROUPS, CHUNKS, CHUNK * B, B), BF16),
            pltpu.VMEM((GROUPS, ROWS, B), BF16),
            pltpu.VMEM((GROUPS, ROWS * B, WIDE), BF16),
            pltpu.VMEM((WIDE, ROWS * B), BF16),
            pltpu.VMEM((ROWS, B), F32),
            pltpu.VMEM((GROUPS, 2, 2, OUT, WIDE), F32),
            pltpu.VMEM((GROUPS, 2, OUT, WIDE), F32),
            pltpu.VMEM((GROUPS, 2, OUT, WIDE), BF16),
            pltpu.VMEM((CHIPS, OUT, WIDE), BF16),
            pltpu.VMEM((OUT, WIDE), F32),
            pltpu.SMEM((ROWS, K), jnp.int32),
            pltpu.SMEM((1, ROWS), jnp.int32),
            dma((2,)),
            dma((2,)),
            dma((4,)),
            dma((6, 2)),
            dma((6, 2)),
            dma((2, 4, CHUNKS)),
            dma((2, 4, CHUNKS)),
            dma((2, 4)),
            dma((2, 4)),
            dma((GROUPS,)),
            dma((GROUPS,)),
            dma((GROUPS, 2)),
            dma((CHIPS,)),
        ],
        compiler_params=pltpu.CompilerParams(
            collective_id=0, has_side_effects=True, vmem_limit_bytes=60 * 2**20
        ),
    )(
        fcol,
        zcol.reshape(1, ROWS),
        fblocks.reshape(ROWS, K * B, B),
        zblocks.reshape(ROWS * B, B),
    )


def solution(mesh):
    in_specs = (
        P("rows", None, None, None),
        P("rows", None),
        P("rows", "cols", None, None),
        P("rows", "cols"),
    )
    out_specs = P("rows", "cols")
    return jax.shard_map(body, mesh=mesh, in_specs=in_specs, out_specs=out_specs, check_vma=False)
```

```python
import jax
import jax.numpy as jnp
from jax import lax
from jax.experimental import pallas as pl
from jax.experimental.pallas import tpu as pltpu
from jax.sharding import PartitionSpec as P

B = 128
K = 20
CB = 2
ROWS = 16
CHIPS = 16
GROUPS = 8
NB = 512
SLOTS = 7
OWN = 3
HALF = ROWS // 2
WIDE = CB * B
OUT = 64
CHUNKS = 4
CHUNK = ROWS // CHUNKS
LAST = GROUPS - 1
ORDER = (0, -1, 1, -2, 2, -3, 3, 4)
MESH = pl.DeviceIdType.MESH
F32 = jnp.float32
BF16 = jnp.bfloat16


def kernel(
    fcol_hbm,
    zcol_hbm,
    f_hbm,
    z_hbm,
    out,
    fv,
    halo,
    zexp,
    ring,
    tags,
    wide,
    turned,
    masks,
    part,
    other,
    chip_sum,
    arrived,
    total,
    fcol,
    zcol,
    small_sem,
    z_sem,
    f_sem,
    halo_send,
    halo_recv,
    ring_send,
    ring_recv,
    tag_send,
    tag_recv,
    pair_send,
    pair_recv,
    sum_send,
    sum_recv,
    last_send,
    last_recv,
):
    r = lax.axis_index("rows")
    z = lax.axis_index("cols")
    m = lax.div(r, 2)
    q = lax.rem(r, 2)
    s = 2 * q - 1

    def chip(step):
        return lax.rem(m + step + 2 * CHIPS, CHIPS)

    def group(step):
        return lax.rem(z + step + 2 * GROUPS, GROUPS)

    sibling = (r - s, z)

    load_z = []
    for half in range(2):
        load_z.append(
            pltpu.make_async_copy(
                z_hbm.at[pl.ds(half * HALF * B, HALF * B)],
                halo.at[OWN, half, pl.ds(0, HALF * B)],
                z_sem.at[half],
            )
        )
        load_z[-1].start()
    load_zcol = pltpu.make_async_copy(zcol_hbm, zcol, small_sem.at[0])
    load_zcol.start()
    load_fcol = pltpu.make_async_copy(fcol_hbm, fcol, small_sem.at[1])
    load_fcol.start()
    load_f = []
    for g in range(4):
        rows = pl.ds(4 * g, 4)
        load_f.append(pltpu.make_async_copy(f_hbm.at[rows], fv.at[rows], f_sem.at[g]))
        load_f[-1].start()

    barrier = pltpu.get_barrier_semaphore()
    peers = [(r, group(1)), (r, group(-1)), sibling, (2 * chip(s) + 1 - q, z)]
    peers += [(2 * chip(j) + q, z) for j in range(1, CHIPS)]
    for peer in peers:
        pl.semaphore_signal(barrier, inc=1, device_id=peer, device_id_type=MESH)

    def remote(src, dst, send, recv, device):
        return pltpu.make_async_remote_copy(
            src_ref=src, dst_ref=dst, send_sem=send, recv_sem=recv,
            device_id=device, device_id_type=MESH,
        )

    sent = []

    def go(copy):
        copy.start()
        sent.append(copy)

    def drain(count):
        for copy in sent[:count]:
            copy.wait_send()
        del sent[:count]

    def ring_copy(sense, distance, chunk):
        n = group(-sense * (distance - 1))
        at = (0 if sense == 1 else 1, distance - 1, chunk)
        if distance == 1:
            source = z_hbm.at[pl.ds(chunk * CHUNK * B, CHUNK * B)]
        else:
            source = ring.at[n, chunk]
        return remote(
            source, ring.at[n, chunk], ring_send.at[at], ring_recv.at[at], (r, group(sense))
        )

    def ring_wait(sense, distance, chunk):
        n = group(-sense * distance)
        at = (0 if sense == 1 else 1, distance - 1, chunk)
        remote(
            ring.at[n, chunk], ring.at[n, chunk], ring_send.at[at], ring_recv.at[at],
            (r, group(sense)),
        ).wait_recv()

    def tag_copy(sense, distance):
        n = group(-sense * (distance - 1))
        at = (0 if sense == 1 else 1, distance - 1)
        return remote(
            tags.at[n], tags.at[n], tag_send.at[at], tag_recv.at[at], (r, group(sense))
        )

    def tag_wait(sense, distance):
        n = group(-sense * distance)
        at = (0 if sense == 1 else 1, distance - 1)
        remote(
            tags.at[n], tags.at[n], tag_send.at[at], tag_recv.at[at], (r, group(sense))
        ).wait_recv()

    pl.semaphore_wait(barrier, len(peers))
    go(ring_copy(1, 1, 0))
    go(ring_copy(-1, 1, CHUNKS - 1))

    load_zcol.wait()
    load_fcol.wait()
    row_of = lax.broadcasted_iota(jnp.int32, (ROWS, B), 0)

    def mask_tile(first):
        tile = jnp.zeros((ROWS, B), F32)
        for i in range(first, ROWS):
            tile = jnp.where(row_of == i - first, zcol[0, i].astype(F32), tile)
        return tile.astype(BF16)

    tags[z] = mask_tile(0)
    go(tag_copy(1, 1))
    go(tag_copy(-1, 1))
    halo[OWN, 0, pl.ds(HALF * B, ROWS)] = mask_tile(0)
    halo[OWN, 1, pl.ds(HALF * B, ROWS)] = mask_tile(HALF)
    for half in range(2):
        load_z[half].wait()

    def halo_copy(step, order, src_slot, dst_slot, device, core=q):
        half = core if order == 0 else 1 - core
        return remote(
            halo.at[src_slot, half], halo.at[dst_slot, half],
            halo_send.at[step, order], halo_recv.at[step, order], device,
        )

    def halo_wait(step, order, slot):
        halo_copy(step, order, slot, slot, sibling, q if step < 2 else 1 - q).wait_recv()

    for order in range(2):
        go(halo_copy(0, order, OWN, 1, (2 * chip(1) + q, z)))
        go(halo_copy(1, order, OWN, 5, (2 * chip(-1) + q, z)))
    for order in range(2):
        go(halo_copy(2, order, OWN, 3 + s, sibling))
    for j in range(1, CHUNKS):
        go(ring_copy(1, 1, j))
        go(ring_copy(-1, 1, CHUNKS - 1 - j))

    def expand_slot(slot, half):
        masks[...] = halo[slot, half, pl.ds(HALF * B, ROWS)].astype(F32)

        @pl.loop(0, HALF)
        def _(j):
            block = halo[slot, half, pl.ds(pl.multiple_of(j * B, B), B)]
            second = masks[pl.ds(j, 1), :].astype(BF16)
            at = slot * ROWS + half * HALF + j
            zexp[at, :, 0:B] = block * (1 - second)
            zexp[at, :, B:WIDE] = block * second

    def expand_both(slot):
        expand_slot(slot, 0)
        expand_slot(slot, 1)

    expand_both(OWN)
    halo_wait(2, 0, 3 - s)
    halo_wait(2, 1, 3 - s)
    expand_both(3 - s)

    def expand_chunk(t, chunk):
        n = group(ORDER[t])
        masks[...] = tags[n].astype(F32)

        @pl.loop(0, CHUNK)
        def _(j):
            block = ring[n, chunk, pl.ds(pl.multiple_of(j * B, B), B)]
            second = masks[pl.ds(chunk * CHUNK + j, 1), :].astype(BF16)
            rows = pl.ds(pl.multiple_of((chunk * CHUNK + j) * B, B), B)
            wide[t, rows, 0:B] = block * (1 - second)
            wide[t, rows, B:WIDE] = block * second

    def forward(distance, j):
        both = ((1, j), (-1, CHUNKS - 1 - j))
        for sense, chunk in both:
            ring_wait(sense, distance, chunk)
            if distance < 3 or (distance == 3 and j < CHUNKS // 2):
                go(ring_copy(sense, distance + 1, chunk))
        if j == 0:
            for sense, chunk in both:
                tag_wait(sense, distance)
                if distance < 3 or sense == 1:
                    go(tag_copy(sense, distance + 1))
        expand_chunk(2 * distance - 1, j)
        expand_chunk(2 * distance, CHUNKS - 1 - j)

    def halo_forward(order):
        halo_wait(0, order, 1)
        halo_wait(1, order, 5)
        go(halo_copy(5, order, 3 - 2 * s, 3 - 3 * s, (2 * chip(s) + 1 - q, z)))
        go(halo_copy(3, order, 1, 1 + s, sibling))
        go(halo_copy(4, order, 5, 5 + s, sibling))

    forward(1, 0)
    halo_forward(0)
    forward(1, 1)
    forward(1, 2)
    halo_forward(1)
    forward(1, 3)
    expand_both(1)
    expand_both(5)
    for order in range(2):
        halo_wait(3, order, 1 - s)
        halo_wait(4, order, 5 - s)
    expand_both(1 - s)
    expand_both(5 - s)

    first_row = (r - OWN) * ROWS

    def place(column):
        return jnp.minimum(lax.rem(column - first_row + NB, NB), SLOTS * ROWS - 1)

    def product_row(i):
        left = jnp.concatenate([fv[i, pl.ds(k * B, B)] for k in range(K)], axis=1)
        right = jnp.concatenate([zexp[place(fcol[i, k])] for k in range(K)], axis=0)
        acc = jnp.dot(left, right, preferred_element_type=F32)
        rows = pl.ds(pl.multiple_of(i * B, B), B)
        for c in range(CB):
            turned[c * B:(c + 1) * B, rows] = jnp.transpose(acc[:, c * B:(c + 1) * B].astype(BF16))

    def product_rows(first):
        for i in range(4):
            product_row(first + i)

    for g in range(4):
        load_f[g].wait()
    near = HALF * (1 - q)
    halo_wait(5, 0, 3 + 3 * s)
    expand_slot(3 + 3 * s, 1 - q)
    product_rows(near)
    forward(2, 0)
    product_rows(near + 4)
    forward(2, 1)
    halo_wait(5, 1, 3 + 3 * s)
    expand_slot(3 + 3 * s, q)
    product_rows(HALF * q)
    forward(2, 2)
    product_rows(HALF * q + 4)
    forward(2, 3)

    def group_of(t):
        return group(ORDER[t])

    pair_copies = []

    def last_copy(h):
        return remote(
            part.at[LAST, 1 - q, h], other.at[LAST, h], last_send.at[h], last_recv.at[h], sibling
        )

    def last_window():
        accs = [jnp.zeros((WIDE, B), F32)] * 2
        for j in range(CHUNKS // 2):
            both = ((1, j), (-1, CHUNKS - 1 - j))
            for sense, chunk in both:
                ring_wait(sense, 4, chunk)
                expand_chunk(LAST, chunk)
            for h in range(2):
                for _, chunk in both:
                    rows = pl.ds(chunk * CHUNK * B, CHUNK * B)
                    accs[h] += jnp.dot(
                        turned[:, rows], wide[LAST, rows, h * B:(h + 1) * B],
                        preferred_element_type=F32,
                    )
                if j == CHUNKS // 2 - 1:
                    product = jnp.transpose(accs[h])
                    for core in range(2):
                        part[LAST, core, h] = product[core * OUT:(core + 1) * OUT]
                    go(last_copy(h))

    def window(t):
        right = wide[t]
        if t == 0:
            right = zexp[OWN * ROWS:(OWN + 1) * ROWS].reshape(ROWS * B, WIDE)
        product = jnp.dot(turned[...], right, preferred_element_type=F32)
        product = jnp.transpose(product)
        for b in range(4):
            part[t, b % 2, b // 2] = product[b * OUT:(b + 1) * OUT]
        copy = remote(
            part.at[t, 1 - q], other.at[t], pair_send.at[t], pair_recv.at[t], sibling
        )
        pair_copies.append(copy)
        go(copy)

    def sum_copy(t, h):
        d = 2 * group_of(t) + h
        return d, remote(
            chip_sum.at[t, h], arrived.at[m], sum_send.at[t, h], sum_recv.at[m],
            (2 * d + q, z),
        )

    def finish(t):
        if t != LAST:
            pair_copies[t].wait_recv()
        for h in range(2):
            if t == LAST:
                last_copy(h).wait_recv()
            both = part[t, q, h] + other[t, h]
            chip_sum[t, h] = both.astype(BF16)
            d, copy = sum_copy(t, h)

            @pl.when(d == m)
            def _():
                total[...] = both

            @pl.when(d != m)
            def _():
                copy.start()

    window(0)
    early = len(sent)
    forward(3, 0)
    window(1)
    finish(0)
    window(2)
    forward(3, 1)
    finish(1)
    window(3)
    finish(2)
    window(4)
    finish(3)
    finish(4)
    forward(3, 2)
    forward(3, 3)
    window(5)
    window(6)
    finish(5)
    finish(6)
    drain(early)
    tag_wait(1, 4)
    last_window()
    finish(7)

    acc = total[...]
    for j in range(1, CHIPS):
        source = chip(j)
        remote(
            arrived.at[source], arrived.at[source], sum_send.at[0, 0], sum_recv.at[source], sibling
        ).wait_recv()
        acc += arrived[source].astype(F32)
    out[...] = acc

    drain(len(sent))
    for t in range(GROUPS):
        for h in range(2):
            d, copy = sum_copy(t, h)

            @pl.when(d != m)
            def _():
                copy.wait_send()


def body(fblocks, fcol, zblocks, zcol):
    dma = pltpu.SemaphoreType.DMA
    return pl.pallas_call(
        kernel,
        out_shape=pltpu.VMEM((OUT, WIDE), F32),
        in_specs=[pl.BlockSpec(memory_space=pl.ANY)] * 4,
        out_specs=pl.BlockSpec(memory_space=pltpu.VMEM),
        scratch_shapes=[
            pltpu.VMEM((ROWS, K * B, B), BF16),
            pltpu.VMEM((SLOTS, 2, HALF * B + ROWS, B), BF16),
            pltpu.VMEM((SLOTS * ROWS, B, WIDE), BF16),
            pltpu.VMEM((GROUPS, CHUNKS, CHUNK * B, B), BF16),
            pltpu.VMEM((GROUPS, ROWS, B), BF16),
            pltpu.VMEM((GROUPS, ROWS * B, WIDE), BF16),
            pltpu.VMEM((WIDE, ROWS * B), BF16),
            pltpu.VMEM((ROWS, B), F32),
            pltpu.VMEM((GROUPS, 2, 2, OUT, WIDE), F32),
            pltpu.VMEM((GROUPS, 2, OUT, WIDE), F32),
            pltpu.VMEM((GROUPS, 2, OUT, WIDE), BF16),
            pltpu.VMEM((CHIPS, OUT, WIDE), BF16),
            pltpu.VMEM((OUT, WIDE), F32),
            pltpu.SMEM((ROWS, K), jnp.int32),
            pltpu.SMEM((1, ROWS), jnp.int32),
            dma((2,)),
            dma((2,)),
            dma((4,)),
            dma((6, 2)),
            dma((6, 2)),
            dma((2, 4, CHUNKS)),
            dma((2, 4, CHUNKS)),
            dma((2, 4)),
            dma((2, 4)),
            dma((GROUPS,)),
            dma((GROUPS,)),
            dma((GROUPS, 2)),
            dma((CHIPS,)),
            dma((2,)),
            dma((2,)),
        ],
        compiler_params=pltpu.CompilerParams(
            collective_id=0, has_side_effects=True, vmem_limit_bytes=60 * 2**20
        ),
    )(
        fcol,
        zcol.reshape(1, ROWS),
        fblocks.reshape(ROWS, K * B, B),
        zblocks.reshape(ROWS * B, B),
    )


def solution(mesh):
    in_specs = (
        P("rows", None, None, None),
        P("rows", None),
        P("rows", "cols", None, None),
        P("rows", "cols"),
    )
    out_specs = P("rows", "cols")
    return jax.shard_map(body, mesh=mesh, in_specs=in_specs, out_specs=out_specs, check_vma=False)
```
